32 devices in a mesh: parts: 2 (over x), dev: 16 (over z, y, core).
Axes of the slice: x: 2, y: 2, z: 4, core: 2. Of those that a mesh axis runs over, the one named last changes fastest.
Arguments:
- tokens: bfloat16 [256, 3072], P(('parts', 'dev')), parts along dimension 0, may hold values from -6 to 6
- grad_out: bfloat16 [256, 3072], P(('parts', 'dev')), parts along dimension 0, may hold values from -6 to 6
- expert_ids: int32 [256, 2], P(('parts', 'dev')), parts along dimension 0, may hold values from 0 to 7, all different within a row; in each aligned block of 8 rows (0 to 7, 8 to 15, ...) at most 4 rows name the same one
- gate_probs: float32 [256, 2], P(('parts', 'dev')), parts along dimension 0, may hold values from 0.1 to 1
- device_expert: int32 [16], replicated, may hold values from 0 to 3, as said below
- w_in: bfloat16 [3072, 2, 4096], P(None, None, 'dev'), may hold values from -0.109375 to 0.109375
- w_down: bfloat16 [4096, 3072], P('dev'), may hold values from -0.1875 to 0.1875
Outputs:
- grad_tokens: bfloat16 [256, 3072], P(('parts', 'dev')), parts along dimension 0
- grad_gates: float32 [256, 2], P(('parts', 'dev')), parts along dimension 0
- grad_w_in: bfloat16 [6144, 2, 4096], P('parts', None, 'dev'), parts along dimension 0
- grad_w_down: bfloat16 [8192, 3072], P(('parts', 'dev')), parts along dimension 0
The draws below stay inside these ranges and needn't reach their ends.
There are 2 independent parts, one for each index of `parts`. The reference program is written for one: setup_inputs(seed, part) draws one part's arguments, and reference() takes and returns one part's arrays. A program takes and returns all parts, laid end to end along the dimension named above; an argument that names none is the same for every part. Nothing has to cross between parts.
Inputs may be any that keep to these rules, and one draw needn't show every extreme that they name: `expert_ids`: each token names 2 different experts; among the 8 tokens of one device no expert is named more than 4 times. `device_expert`: each of the 4 experts is held by a multiple of 2 devices, at least that many, at drawn positions along the axis.
All inputs are finite; a program needn't handle non-finite values.
Results may differ from the reference program's by a relative error of at most 0.0065.
Values may be sent and summed in bfloat16 or wider, within the bound.
No kernel may reach another device: no remote copies, remote signals or barrier semaphores. Data moves between devices by JAX's collectives and lax.ppermute only.
A program may use at most 64 MiB of HBM per device.

```python
import math
import jax
import jax.numpy as jnp
import numpy as np
from jax import lax

D = 3072
EXPERTS = 8
TOP = 2
EXP_WIN = 4
HID_DEV = 256
TOK_DEV = 8
MOST = 4
TOKENS = 128
HIDDEN_SIZE = 4096
N_DEV = 16


def draw_device_expert(key, part):
    key = jax.random.fold_in(key, 11)
    first_key, second_key = jax.random.split(key)
    ordering = jax.random.permutation(first_key, N_DEV)
    group_of = ordering // (N_DEV // 8)
    cut_points = jax.random.permutation(second_key, 7)[:3] + 1
    return jnp.sum((group_of[:, None] >= cut_points[None, :]).astype(jnp.int32), 1).astype(jnp.int32)


def shard_levels(rng, dims, cuts, least, high):
    loudness = 1.0
    for position, blocks in cuts:
        heights = jax.random.uniform(jax.random.fold_in(jax.random.fold_in(rng, 6), position), (blocks,), jnp.float32, least / len(cuts), high / len(cuts))
        loudness = loudness * jnp.repeat(jnp.exp(heights), dims[position] // blocks).reshape((-1,) + (1,) * (len(dims) - 1 - position))
    return loudness


def shared_out(stream_key, own, number, rows, number_of, top, most, lean):
    sequence = jax.random.permutation(stream_key, number_of)
    heavy_load, ordinary = portions_of(number_of, rows * top, most, lean, True), portions_of(number_of, rows * top, most, lean, False)
    places = jnp.arange(number_of)

    def named(sizes, rotation):
        used = int((sizes > 0).sum())
        fixed = max(1, used // 4)
        shifted = fixed + (places - fixed + rotation * (used - fixed)) % max(1, number_of - fixed)
        return jnp.zeros((number_of,), jnp.int32).at[sequence[jnp.where(places < fixed, places, shifted)]].set(jnp.asarray(sizes, jnp.int32))

    sizes = jnp.where(number % 4 == 0, named(heavy_load, number // 4), named(ordinary, number - number // 4 - 1))
    mixed = jax.random.permutation(jax.random.fold_in(own, 3), number_of)
    giver, taker = mixed[0:number_of // 2 * 2:2], mixed[1:number_of // 2 * 2:2]
    margin = jnp.minimum(sizes[giver] - 1, most - sizes[taker]) // 2
    margin = jnp.where((giver == sequence[0]) | (taker == sequence[0]) | (sizes[taker] == 0), 0, jnp.maximum(margin, 0))
    shifted = jax.random.randint(jax.random.fold_in(own, 4), (number_of // 2,), 0, 1 << 20) % (margin + 1)
    sizes = sizes.at[giver].add(-shifted).at[taker].add(shifted)
    labels = jnp.searchsorted(jnp.cumsum(sizes), jnp.arange(rows * top), side="right").astype(jnp.int32)
    grid = labels.reshape(top, rows).T
    grid = grid[jax.random.permutation(jax.random.fold_in(own, 1), rows)]
    rotation = jax.random.randint(jax.random.fold_in(own, 2), (rows, 1), 0, top)
    return jnp.take_along_axis(grid, (jnp.arange(top)[None, :] + rotation) % top, axis=1)


def portions_of(count, total, limit, skew, full):
    portions = [(1 << 20) // math.isqrt(standing ** skew) + 1 for standing in range(1, count + 1)]
    largest = limit if full else min(limit, max(-(-total // count), total * portions[0] // sum(portions)))
    least = 1 if total - largest >= count - 1 else 0
    holding, spare = [largest] + [least] * (count - 1), total - largest - least * (count - 1)
    while spare > 0:
        free = [i for i in range(1, count) if holding[i] < largest] or [i for i in range(1, count) if holding[i] < limit]
        mass, left = sum([portions[i] for i in free]), spare
        for i in free:
            extra = min(limit - holding[i], max(1, left * portions[i] // mass), spare)
            holding[i] = holding[i] + extra
            spare = spare - extra
    return np.array(holding)


def scatter_about(rng, extent, spread, bound, pieces=(), kind=jnp.bfloat16):
    array = spread * jax.random.normal(rng, extent, jnp.float32)
    if pieces:
        array = array * shard_levels(rng, extent, pieces, -0.22, 0.18)
    return jnp.clip(array, -bound, bound).astype(kind)


def setup_inputs(seed: int = 0, part: int = 0) -> dict:
    keys = jax.random.split(jax.random.key(seed), 8)
    own_keys = jax.random.split(jax.random.fold_in(keys[7], part), 8)
    tokens = scatter_about(own_keys[0], (TOKENS, D), 1.0, 6.0, ((0, 16),))
    grad_out = scatter_about(own_keys[1], (TOKENS, D), 1.0, 6.0, ((0, 16),))
    expert_ids_keys = jax.random.split(jax.random.fold_in(own_keys[2], 1), TOKENS // TOK_DEV)
    expert_ids_turns = jax.random.permutation(jax.random.fold_in(own_keys[2], 3), TOKENS // TOK_DEV)
    expert_ids = jax.vmap(lambda own, number: shared_out(jax.random.fold_in(own_keys[2], 2), own, number, TOK_DEV, EXPERTS, TOP, MOST, 2))(expert_ids_keys, expert_ids_turns).reshape((TOKENS, TOP))
    gate_probs = jnp.clip(0.1 + 0.9 * jax.random.uniform(own_keys[3], (TOKENS, TOP), jnp.float32) ** shard_levels(own_keys[3], (TOKENS, TOP), ((0, 16),), -0.2, 0.2), 0.1, 1.0)
    device_expert = draw_device_expert(jax.random.fold_in(keys[7], 71), part)
    w_in = scatter_about(keys[5], (D, 2, HIDDEN_SIZE), D ** -0.5, 0.109375, ((2, 16),))
    w_down = scatter_about(keys[6], (HIDDEN_SIZE, D), (HIDDEN_SIZE // 4) ** -0.5, 0.1875, ((0, 16),))
    return {"tokens": tokens, "grad_out": grad_out, "expert_ids": expert_ids, "gate_probs": gate_probs, "device_expert": device_expert, "w_in": w_in, "w_down": w_down}


def reference(tokens, grad_out, expert_ids, gate_probs, device_expert, w_in, w_down):
    experts = jnp.arange(EXP_WIN, dtype=jnp.int32)
    matched = (expert_ids[:, :, None] == experts[None, None, :]).astype(jnp.float32)
    routed = jnp.sum(matched, 1)
    weights = jnp.sum(gate_probs[:, :, None] * matched, 1)
    blocks_in = jnp.transpose(w_in.reshape(D, 2, N_DEV, HID_DEV), (2, 0, 1, 3))
    blocks_down = w_down.reshape(N_DEV, HID_DEV, D)

    def block_step(carry, inputs):
        token_acc, gate_acc = carry
        slice_in, slice_down, owner = inputs
        expert_hot = (experts == owner).astype(jnp.float32)
        mask_rows = jnp.sum(routed * expert_hot[None, :], 1)
        prob_rows = jnp.sum(weights * expert_hot[None, :], 1)
        gate_pre = jnp.dot(tokens, slice_in[:, 0, :], preferred_element_type=jnp.float32)
        up_pre = jnp.dot(tokens, slice_in[:, 1, :], preferred_element_type=jnp.float32)
        logistic = jax.nn.sigmoid(gate_pre)
        activated = gate_pre * logistic
        hidden = (activated * up_pre).astype(jnp.bfloat16)
        hidden_back = jnp.dot(grad_out, slice_down.T, preferred_element_type=jnp.float32)
        gate_part = mask_rows * jnp.sum(hidden.astype(jnp.float32) * hidden_back, 1)
        hidden_grad = prob_rows[:, None] * hidden_back
        grad_gate_pre = (hidden_grad * up_pre * logistic * (1.0 + gate_pre * (1.0 - logistic))).astype(jnp.bfloat16)
        grad_up_pre = (hidden_grad * activated).astype(jnp.bfloat16)
        token_term = jnp.dot(grad_gate_pre, slice_in[:, 0, :].T, preferred_element_type=jnp.float32)
        token_term = token_term + jnp.dot(grad_up_pre, slice_in[:, 1, :].T, preferred_element_type=jnp.float32)
        weight_gate = jnp.dot(tokens.T, grad_gate_pre, preferred_element_type=jnp.float32)
        weight_up = jnp.dot(tokens.T, grad_up_pre, preferred_element_type=jnp.float32)
        weight_in = jnp.stack([weight_gate, weight_up], 1).astype(jnp.bfloat16)
        scaled = (prob_rows[:, None] * grad_out.astype(jnp.float32)).astype(jnp.bfloat16)
        weight_down = jnp.dot(hidden.T, scaled, preferred_element_type=jnp.float32).astype(jnp.bfloat16)
        new_carry = (token_acc + token_term, gate_acc + gate_part[:, None] * expert_hot[None, :])
        return new_carry, (weight_in, weight_down)

    start_carry = (jnp.zeros((TOKENS, D), jnp.float32), jnp.zeros((TOKENS, EXP_WIN), jnp.float32))
    (token_acc, gate_acc), (stack_in, stack_down) = lax.scan(block_step, start_carry, (blocks_in, blocks_down, device_expert))
    grad_tokens = token_acc.astype(jnp.bfloat16)
    grad_gates = jnp.sum(gate_acc[:, None, :] * matched, 2)
    grad_w_in = jnp.transpose(stack_in, (1, 2, 0, 3)).reshape(D, 2, N_DEV * HID_DEV)
    grad_w_down = stack_down.reshape(N_DEV * HID_DEV, D)
    return grad_tokens, grad_gates, grad_w_in, grad_w_down
```

```python
import functools

import jax
import jax.numpy as jnp
from jax import lax
from jax.experimental import pallas as pl
from jax.experimental.pallas import tpu as pltpu
from jax.sharding import PartitionSpec as P

EXP_WIN = 4
META = 128
BF = jnp.bfloat16
F32 = jnp.float32
VMEM = pl.BlockSpec(memory_space=pltpu.VMEM)
SMEM = pl.BlockSpec(memory_space=pltpu.SMEM)
NT = (((1,), (1,)), ((), ()))
TN = (((0,), (0,)), ((), ()))


def params():
    return pltpu.CompilerParams(vmem_limit_bytes=48 << 20)


def xor_swap(value, bit):
    n = lax.axis_size("dev")
    return lax.ppermute(value, "dev", [(i, i ^ bit) for i in range(n)])


def xor_bits(n):
    bits = []
    bit = n // 2
    while bit:
        bits.append(bit)
        bit //= 2
    return bits


def pack_kernel(tok_ref, grad_ref, ids_ref, prob_ref, out_ref):
    rows, width = tok_ref.shape
    out_ref[:, :width] = tok_ref[...]
    out_ref[:, width : 2 * width] = grad_ref[...]
    top = ids_ref.shape[0]
    diag = lax.broadcasted_iota(jnp.int32, (rows, rows), 0) == lax.broadcasted_iota(
        jnp.int32, (rows, rows), 1
    )
    lane = lax.broadcasted_iota(jnp.int32, (rows, META), 1)
    expert = lane % EXP_WIN
    flag = jnp.zeros((rows, META), F32)
    prob = jnp.zeros((rows, META), F32)
    for k in range(top):
        ids = jnp.broadcast_to(ids_ref[k : k + 1, :].astype(F32), (rows, rows))
        val = jnp.broadcast_to(prob_ref[k : k + 1, :], (rows, rows))
        ids = jnp.sum(jnp.where(diag, ids, 0.0), 1, keepdims=True)
        val = jnp.sum(jnp.where(diag, val, 0.0), 1, keepdims=True)
        hit = expert.astype(F32) == ids
        flag = jnp.where(hit, 1.0, flag)
        prob = prob + jnp.where(hit, val, 0.0)
    high = prob.astype(BF).astype(F32)
    mid = (prob - high).astype(BF).astype(F32)
    low = prob - high - mid
    part = lane // EXP_WIN
    meta = jnp.where(part == 0, flag, 0.0)
    meta = jnp.where(part == 1, high, meta)
    meta = jnp.where(part == 2, mid, meta)
    meta = jnp.where(part == 3, low, meta)
    out_ref[:, 2 * width :] = meta.astype(BF)


def split_kernel(w_ref, out_ref):
    hid = w_ref.shape[2]
    block = w_ref[...]
    out_ref[:, :hid] = block[:, 0, :]
    out_ref[:, hid:] = block[:, 1, :]


def split_weights(w_in, block=512):
    d, two, hid = w_in.shape
    return pl.pallas_call(
        split_kernel,
        grid=(d // block,),
        in_specs=[pl.BlockSpec((block, two, hid), lambda i: (i, 0, 0))],
        out_specs=pl.BlockSpec((block, two * hid), lambda i: (i, 0)),
        out_shape=jax.ShapeDtypeStruct((d, two * hid), BF),
        compiler_params=params(),
        cost_estimate=pl.CostEstimate(
            flops=0, bytes_accessed=30 * d * two * hid, transcendentals=0
        ),
    )(w_in)


def put_gate(out_ref, value, expert, width):
    rows = value.shape[0]
    lane = lax.broadcasted_iota(jnp.int32, (rows, META), 1)
    high = value.astype(BF).astype(F32)
    low = value - high
    pair = jnp.where(lane == expert, high, 0.0)
    pair = jnp.where(lane == expert + EXP_WIN, low, pair)
    out_ref[:, width:] = pair.astype(out_ref.dtype)


def token_part(pre, w_ref, out_ref, width, step=768):
    for c in range(0, width, step):
        out_ref[:, c : c + step] = lax.dot_general(
            pre, w_ref[c : c + step, :], NT, preferred_element_type=F32
        ).astype(out_ref.dtype)


def main_kernel(n, owner_ref, me_ref, *refs):
    pieces, refs = refs[:n], refs[n:]
    w_ref, down_ref, tok_ref, scaled_ref, pre_ref, hid_ref, gate_ref, send_ref, grad_ref = refs
    rows = pieces[0].shape[0]
    width = down_ref.shape[1]
    hid = down_ref.shape[0]
    expert = owner_ref[me_ref[0]]
    metas = []
    for i in range(0, n, 2):
        pair = [pieces[i][...].astype(F32), pieces[i + 1][...].astype(F32)]
        both = jnp.concatenate(pair, 0)
        here = pl.ds(i * rows, 2 * rows)
        tok_ref[here, :] = both[:, :width].astype(BF)
        grad_ref[here, :] = both[:, width : 2 * width].astype(BF)
        metas.append(both[:, 2 * width :])
    meta = jnp.concatenate(metas, 0)
    lane = lax.broadcasted_iota(jnp.int32, meta.shape, 1)
    routed = jnp.sum(jnp.where(lane == expert, meta, 0.0), 1, keepdims=True)
    prob = jnp.sum(
        jnp.where((lane >= EXP_WIN) & (lane % EXP_WIN == expert), meta, 0.0), 1, keepdims=True
    )
    projected = jnp.dot(tok_ref[...], w_ref[...], preferred_element_type=F32)
    gate, up = projected[:, :hid], projected[:, hid:]
    back = lax.dot_general(grad_ref[...], down_ref[...], NT, preferred_element_type=F32)
    logistic = jax.nn.sigmoid(gate)
    activated = gate * logistic
    hidden = (activated * up).astype(BF)
    hid_ref[...] = hidden
    gate_sum = routed * jnp.sum(hidden.astype(F32) * back, 1, keepdims=True)
    hidden_grad = prob * back
    pre_gate = hidden_grad * up * logistic * (1.0 + gate * (1.0 - logistic))
    pre_ref[:, :hid] = pre_gate.astype(BF)
    pre_ref[:, hid:] = (hidden_grad * activated).astype(BF)
    gate_ref[...] = jnp.broadcast_to(gate_sum, gate_ref.shape)
    half = n * rows // 2
    put_gate(send_ref, gate_sum[half:], expert, width)
    token_part(pre_ref[half:, :], w_ref, send_ref, width)
    scaled_ref[...] = (prob * grad_ref[...].astype(F32)).astype(BF)


def own_kernel(owner_ref, me_ref, pre_ref, w_ref, gate_ref, out_ref):
    half = out_ref.shape[0]
    width = w_ref.shape[0]
    put_gate(out_ref, gate_ref[:half, :1], owner_ref[me_ref[0]], width)
    token_part(pre_ref[:half, :], w_ref, out_ref, width)


def add_kernel(own_ref, got_ref, keep_ref, send_ref=None):
    total = own_ref[...] + got_ref[...].astype(F32)
    half = keep_ref.shape[0]
    width = total.shape[1] - META
    keep_ref[...] = total[:half]
    if send_ref is not None:
        send_ref[:, :width] = total[half:, :width].astype(BF)
        tail = total[half:, width:]
        lane = lax.broadcasted_iota(jnp.int32, tail.shape, 1)
        value = tail + pltpu.roll(tail, META - EXP_WIN, 1)
        high = value.astype(BF).astype(F32)
        low = pltpu.roll(value - high, EXP_WIN, 1)
        pair = jnp.where(lane < EXP_WIN, high, jnp.where(lane < 2 * EXP_WIN, low, 0.0))
        send_ref[:, width:] = pair.astype(BF)


def add_step(own, got):
    rows, width = own.shape
    half = rows // 2
    return pl.pallas_call(
        add_kernel,
        in_specs=[VMEM, VMEM],
        out_specs=[VMEM, VMEM],
        out_shape=[
            jax.ShapeDtypeStruct((half, width), F32),
            jax.ShapeDtypeStruct((half, width), BF),
        ],
        compiler_params=params(),
        cost_estimate=pl.CostEstimate(
            flops=rows * width, bytes_accessed=8 * rows * width, transcendentals=0
        ),
    )(own, got)


def last_kernel(own_ref, got_ref, ids_ref, tok_ref, gates_ref):
    total = own_ref[...] + got_ref[...].astype(F32)
    rows = total.shape[0]
    width = total.shape[1] - META
    tok_ref[...] = total[:, :width].astype(BF)
    tail = total[:, width:]
    value = tail + pltpu.roll(tail, META - EXP_WIN, 1)
    lane = lax.broadcasted_iota(jnp.int32, (rows, META), 1)
    diag = lax.broadcasted_iota(jnp.int32, (rows, rows), 0) == lax.broadcasted_iota(
        jnp.int32, (rows, rows), 1
    )
    for k in range(ids_ref.shape[0]):
        ids = jnp.broadcast_to(ids_ref[k : k + 1, :].astype(F32), (rows, rows))
        ids = jnp.sum(jnp.where(diag, ids, 0.0), 1, keepdims=True)
        hit = (lane.astype(F32) == ids) & (lane < EXP_WIN)
        column = jnp.sum(jnp.where(hit, value, 0.0), 1, keepdims=True)
        square = jnp.where(diag, jnp.broadcast_to(column, (rows, rows)), 0.0)
        gates_ref[k : k + 1, :] = jnp.sum(square, 0, keepdims=True)


def win_kernel(tok_ref, pre_ref, out_ref):
    hid = out_ref.shape[2]
    block = lax.dot_general(tok_ref[...], pre_ref[...], TN, preferred_element_type=F32)
    out_ref[:, 0, :] = block[:, :hid].astype(BF)
    out_ref[:, 1, :] = block[:, hid:].astype(BF)


def grad_in(tok, pre, block=256):
    rows, d = tok.shape
    hid = pre.shape[1] // 2
    return pl.pallas_call(
        win_kernel,
        grid=(d // block,),
        in_specs=[
            pl.BlockSpec((rows, block), lambda i: (0, i)),
            pl.BlockSpec((rows, 2 * hid), lambda i: (0, 0)),
        ],
        out_specs=pl.BlockSpec((block, 2, hid), lambda i: (i, 0, 0)),
        out_shape=jax.ShapeDtypeStruct((d, 2, hid), BF),
        compiler_params=params(),
        cost_estimate=pl.CostEstimate(
            flops=4 * rows * d * hid, bytes_accessed=30 * d * hid, transcendentals=0
        ),
    )(tok, pre)


def down_kernel(hid_ref, scaled_ref, out_ref):
    out_ref[...] = lax.dot_general(
        hid_ref[...], scaled_ref[...], TN, preferred_element_type=F32
    ).astype(BF)


def grad_down(hidden, scaled, block=768):
    rows, d = scaled.shape
    hid = hidden.shape[1]
    return pl.pallas_call(
        down_kernel,
        grid=(d // block,),
        in_specs=[
            pl.BlockSpec((rows, hid), lambda i: (0, 0)),
            pl.BlockSpec((rows, block), lambda i: (0, i)),
        ],
        out_specs=pl.BlockSpec((hid, block), lambda i: (0, i)),
        out_shape=jax.ShapeDtypeStruct((hid, d), BF),
        compiler_params=params(),
        cost_estimate=pl.CostEstimate(
            flops=2 * rows * d * hid, bytes_accessed=4 * d * hid, transcendentals=0
        ),
    )(hidden, scaled)


def shards(tokens, grad_out, expert_ids, gate_probs, device_expert, w_in, w_down):
    n = lax.axis_size("dev")
    me = lax.axis_index("dev").astype(jnp.int32).reshape(1)
    rows, width = tokens.shape
    hid = w_down.shape[0]
    ids_t = expert_ids.T
    probs_t = gate_probs.T
    bits = xor_bits(n)

    own = pl.pallas_call(
        pack_kernel,
        in_specs=[VMEM] * 4,
        out_specs=VMEM,
        out_shape=jax.ShapeDtypeStruct((rows, 2 * width + META), BF),
        compiler_params=params(),
    )(tokens, grad_out, ids_t, probs_t)

    held = {0: own}
    order = [0]
    for bit in bits:
        for o in order:
            held[o ^ bit] = xor_swap(held[o], bit)
        order = order + [o ^ bit for o in order]

    w_flat = split_weights(w_in)
    total = n * rows
    half = total // 2
    tok, scaled, pre, hidden, gate, send = pl.pallas_call(
        functools.partial(main_kernel, n),
        in_specs=[SMEM, SMEM] + [VMEM] * (n + 2),
        out_specs=[VMEM] * 6,
        out_shape=[
            jax.ShapeDtypeStruct((total, width), BF),
            jax.ShapeDtypeStruct((total, width), BF),
            jax.ShapeDtypeStruct((total, 2 * hid), BF),
            jax.ShapeDtypeStruct((total, hid), BF),
            jax.ShapeDtypeStruct((total, META), F32),
            jax.ShapeDtypeStruct((half, width + META), BF),
        ],
        scratch_shapes=[pltpu.VMEM((total, width), BF)],
        compiler_params=params(),
    )(device_expert, me, *[held[o] for o in order], w_flat, w_down)

    got = xor_swap(send, 1)
    mine = pl.pallas_call(
        own_kernel,
        in_specs=[SMEM, SMEM] + [VMEM] * 3,
        out_specs=VMEM,
        out_shape=jax.ShapeDtypeStruct((half, width + META), F32),
        compiler_params=params(),
    )(device_expert, me, pre, w_flat, gate)
    for bit in bits[-2::-1]:
        mine, send = add_step(mine, got)
        got = xor_swap(send, bit)

    grad_w_down = grad_down(hidden, scaled)
    grad_w_in = grad_in(tok, pre)
    grad_tokens, gates_t = pl.pallas_call(
        last_kernel,
        in_specs=[VMEM] * 3,
        out_specs=[VMEM] * 2,
        out_shape=[
            jax.ShapeDtypeStruct((rows, width), BF),
            jax.ShapeDtypeStruct((expert_ids.shape[1], rows), F32),
        ],
        compiler_params=params(),
    )(mine, got, ids_t)
    return grad_tokens, gates_t.T, grad_w_in, grad_w_down


def solution(mesh):
    return jax.shard_map(
        shards,
        mesh=mesh,
        in_specs=(
            P(("parts", "dev"), None),
            P(("parts", "dev"), None),
            P(("parts", "dev"), None),
            P(("parts", "dev"), None),
            P(),
            P(None, None, "dev"),
            P("dev", None),
        ),
        out_specs=(
            P(("parts", "dev"), None),
            P(("parts", "dev"), None),
            P("parts", None, "dev"),
            P(("parts", "dev"), None),
        ),
        check_vma=False,
    )
```

```python
import functools

import jax
import jax.numpy as jnp
from jax import lax
from jax.experimental import pallas as pl
from jax.experimental.pallas import tpu as pltpu
from jax.sharding import PartitionSpec as P

EXP_WIN = 4
META = 128
LANES = 128
SIDE = 256
BF = jnp.bfloat16
F32 = jnp.float32
VMEM = pl.BlockSpec(memory_space=pltpu.VMEM)
ANY = pl.BlockSpec(memory_space=pl.ANY)
SMEM = pl.BlockSpec(memory_space=pltpu.SMEM)
NT = (((1,), (1,)), ((), ()))
TN = (((0,), (0,)), ((), ()))


def params(mib=16):
    return pltpu.CompilerParams(vmem_limit_bytes=mib << 20)


def xor_swap(value, bit):
    n = lax.axis_size("dev")
    return lax.ppermute(value, "dev", [(i, i ^ bit) for i in range(n)])


def xor_bits(n):
    bits = []
    bit = n // 2
    while bit:
        bits.append(bit)
        bit //= 2
    return bits


def pack_kernel(tok_ref, grad_ref, ids_ref, prob_ref, out_ref):
    rows, width = tok_ref.shape
    out_ref[:, :width] = tok_ref[...]
    out_ref[:, width : 2 * width] = grad_ref[...]
    top = ids_ref.shape[0]
    diag = lax.broadcasted_iota(jnp.int32, (rows, rows), 0) == lax.broadcasted_iota(
        jnp.int32, (rows, rows), 1
    )
    lane = lax.broadcasted_iota(jnp.int32, (rows, META), 1)
    expert = lane % EXP_WIN
    flag = jnp.zeros((rows, META), F32)
    prob = jnp.zeros((rows, META), F32)
    for k in range(top):
        ids = jnp.broadcast_to(ids_ref[k : k + 1, :].astype(F32), (rows, rows))
        val = jnp.broadcast_to(prob_ref[k : k + 1, :], (rows, rows))
        ids = jnp.sum(jnp.where(diag, ids, 0.0), 1, keepdims=True)
        val = jnp.sum(jnp.where(diag, val, 0.0), 1, keepdims=True)
        hit = expert.astype(F32) == ids
        flag = jnp.where(hit, 1.0, flag)
        prob = prob + jnp.where(hit, val, 0.0)
    high = prob.astype(BF).astype(F32)
    mid = (prob - high).astype(BF).astype(F32)
    low = prob - high - mid
    part = lane // EXP_WIN
    meta = jnp.where(part == 0, flag, 0.0)
    meta = jnp.where(part == 1, high, meta)
    meta = jnp.where(part == 2, mid, meta)
    meta = jnp.where(part == 3, low, meta)
    out_ref[:, 2 * width :] = meta.astype(BF)


def shuffle(group, inverse=False):
    per = SIDE // group
    row = lax.broadcasted_iota(jnp.int32, (SIDE, SIDE), 0)
    col = lax.broadcasted_iota(jnp.int32, (SIDE, SIDE), 1)
    if inverse:
        row, col = col, row
    return (col == (row % per) * group + row // per).astype(BF)


def split_kernel(w_ref, out_ref):
    d, wide = out_ref.shape
    group = wide // LANES
    per = SIDE // group
    tiles = group // 2
    take = shuffle(group)
    for s in range(0, d // per, 2):
        pair = jnp.concatenate(
            [w_ref[s * SIDE : (s + 1) * SIDE, :], w_ref[(s + 1) * SIDE : (s + 2) * SIDE, :]], 1
        )
        rows = jnp.dot(take, pair, preferred_element_type=F32).astype(BF)
        for q in range(group):
            column = (q % 2 * tiles + q // 2) * LANES
            for half in range(2):
                here = (s + half) * per
                out_ref[here : here + per, column : column + LANES] = rows[
                    q * per : (q + 1) * per, half * LANES : (half + 1) * LANES
                ]


def split_weights(w_in, block=512):
    d, two, hid = w_in.shape
    tiles = hid // LANES
    group = two * tiles
    view = w_in.reshape(d, two, tiles, LANES).transpose(0, 2, 1, 3).reshape(d * group, LANES)
    return pl.pallas_call(
        split_kernel,
        grid=(d // block,),
        in_specs=[pl.BlockSpec((block * group, LANES), lambda i: (i, 0))],
        out_specs=pl.BlockSpec((block, two * hid), lambda i: (i, 0)),
        out_shape=jax.ShapeDtypeStruct((d, two * hid), BF),
        compiler_params=params(),
        cost_estimate=pl.CostEstimate(
            flops=2 * d * group * SIDE * LANES, bytes_accessed=8 * d * hid, transcendentals=0
        ),
    )(view)


def put_gate(out_ref, value, expert, width):
    rows = value.shape[0]
    lane = lax.broadcasted_iota(jnp.int32, (rows, META), 1)
    high = value.astype(BF).astype(F32)
    low = value - high
    pair = jnp.where(lane == expert, high, 0.0)
    pair = jnp.where(lane == expert + EXP_WIN, low, pair)
    out_ref[:, width:] = pair.astype(out_ref.dtype)


def token_part(pre, w_ref, out_ref, width, step=768):
    for c in range(0, width, step):
        out_ref[:, c : c + step] = lax.dot_general(
            pre, w_ref[c : c + step, :], NT, preferred_element_type=F32
        ).astype(out_ref.dtype)


def main_kernel(n, owner_ref, *refs):
    pieces, refs = refs[:n], refs[n:]
    w_ref, down_ref, tok_ref, scaled_ref, pre_ref, hid_ref, gate_ref, send_ref, grad_ref = refs
    rows = pieces[0].shape[0]
    width = down_ref.shape[1]
    hid = down_ref.shape[0]
    expert = owner_ref[lax.axis_index("dev")]
    metas = []
    for i in range(0, n, 2):
        pair = [pieces[i][...].astype(F32), pieces[i + 1][...].astype(F32)]
        both = jnp.concatenate(pair, 0)
        here = pl.ds(i * rows, 2 * rows)
        tok_ref[here, :] = both[:, :width].astype(BF)
        grad_ref[here, :] = both[:, width : 2 * width].astype(BF)
        metas.append(both[:, 2 * width :])
    meta = jnp.concatenate(metas, 0)
    lane = lax.broadcasted_iota(jnp.int32, meta.shape, 1)
    routed = jnp.sum(jnp.where(lane == expert, meta, 0.0), 1, keepdims=True)
    prob = jnp.sum(
        jnp.where((lane >= EXP_WIN) & (lane % EXP_WIN == expert), meta, 0.0), 1, keepdims=True
    )
    projected = jnp.dot(tok_ref[...], w_ref[...], preferred_element_type=F32)
    gate, up = projected[:, :hid], projected[:, hid:]
    back = lax.dot_general(grad_ref[...], down_ref[...], NT, preferred_element_type=F32)
    logistic = jax.nn.sigmoid(gate)
    activated = gate * logistic
    hidden = (activated * up).astype(BF)
    hid_ref[...] = hidden
    gate_sum = routed * jnp.sum(hidden.astype(F32) * back, 1, keepdims=True)
    hidden_grad = prob * back
    pre_gate = hidden_grad * up * logistic * (1.0 + gate * (1.0 - logistic))
    pre_ref[:, :hid] = pre_gate.astype(BF)
    pre_ref[:, hid:] = (hidden_grad * activated).astype(BF)
    gate_ref[...] = jnp.broadcast_to(gate_sum, gate_ref.shape)
    half = n * rows // 2
    put_gate(send_ref, gate_sum[half:], expert, width)
    token_part(pre_ref[half:, :], w_ref, send_ref, width)
    scaled_ref[...] = (prob * grad_ref[...].astype(F32)).astype(BF)


def own_kernel(owner_ref, pre_ref, w_ref, gate_ref, out_ref):
    half = out_ref.shape[0]
    width = w_ref.shape[0]
    put_gate(out_ref, gate_ref[:half, :1], owner_ref[lax.axis_index("dev")], width)
    token_part(pre_ref[:half, :], w_ref, out_ref, width)


def add_kernel(own_ref, got_ref, after_ref, keep_ref, send_ref):
    total = own_ref[...] + got_ref[...].astype(F32)
    half = keep_ref.shape[0]
    width = total.shape[1] - META
    keep_ref[...] = total[:half]
    send_ref[:, :width] = total[half:, :width].astype(BF)
    tail = total[half:, width:]
    lane = lax.broadcasted_iota(jnp.int32, tail.shape, 1)
    value = tail + pltpu.roll(tail, META - EXP_WIN, 1)
    high = value.astype(BF).astype(F32)
    low = pltpu.roll(value - high, EXP_WIN, 1)
    pair = jnp.where(lane < EXP_WIN, high, jnp.where(lane < 2 * EXP_WIN, low, 0.0))
    send_ref[:, width:] = pair.astype(BF)


def add_step(own, got, after):
    rows, width = own.shape
    half = rows // 2
    return pl.pallas_call(
        add_kernel,
        in_specs=[VMEM, VMEM, ANY],
        out_specs=[VMEM, VMEM],
        out_shape=[
            jax.ShapeDtypeStruct((half, width), F32),
            jax.ShapeDtypeStruct((half, width), BF),
        ],
        compiler_params=params(),
        cost_estimate=pl.CostEstimate(
            flops=rows * width, bytes_accessed=8 * rows * width, transcendentals=0
        ),
    )(own, got, after)


def last_kernel(own_ref, got_ref, ids_ref, tok_ref, gates_ref):
    total = own_ref[...] + got_ref[...].astype(F32)
    rows = total.shape[0]
    width = total.shape[1] - META
    tok_ref[...] = total[:, :width].astype(BF)
    tail = total[:, width:]
    value = tail + pltpu.roll(tail, META - EXP_WIN, 1)
    lane = lax.broadcasted_iota(jnp.int32, (rows, META), 1)
    diag = lax.broadcasted_iota(jnp.int32, (rows, rows), 0) == lax.broadcasted_iota(
        jnp.int32, (rows, rows), 1
    )
    for k in range(ids_ref.shape[0]):
        ids = jnp.broadcast_to(ids_ref[k : k + 1, :].astype(F32), (rows, rows))
        ids = jnp.sum(jnp.where(diag, ids, 0.0), 1, keepdims=True)
        hit = (lane.astype(F32) == ids) & (lane < EXP_WIN)
        column = jnp.sum(jnp.where(hit, value, 0.0), 1, keepdims=True)
        square = jnp.where(diag, jnp.broadcast_to(column, (rows, rows)), 0.0)
        gates_ref[k : k + 1, :] = jnp.sum(square, 0, keepdims=True)


def win_kernel(tok_ref, pre_ref, out_ref, token_ref):
    wide = pre_ref.shape[1]
    group = wide // LANES
    per = SIDE // group
    tiles = group // 2
    put = shuffle(group, inverse=True)
    block = lax.dot_general(
        tok_ref[...], pre_ref[...], TN, preferred_element_type=F32
    ).astype(BF)
    for s in range(0, tok_ref.shape[1] // per, 2):
        sides = []
        for half in range(2):
            here = (s + half) * per
            sides.append(
                jnp.concatenate(
                    [
                        block[here : here + per, c * LANES : (c + 1) * LANES]
                        for c in [q % 2 * tiles + q // 2 for q in range(group)]
                    ],
                    0,
                )
            )
        rows = jnp.dot(put, jnp.concatenate(sides, 1), preferred_element_type=F32).astype(BF)
        out_ref[s * SIDE : (s + 1) * SIDE, :] = rows[:, :LANES]
        out_ref[(s + 1) * SIDE : (s + 2) * SIDE, :] = rows[:, LANES:]
    token_ref[...] = jnp.zeros_like(token_ref)


def grad_in(tok, pre, block=512):
    rows, d = tok.shape
    hid = pre.shape[1] // 2
    tiles = hid // LANES
    group = 2 * tiles
    out, token = pl.pallas_call(
        win_kernel,
        grid=(d // block,),
        in_specs=[
            pl.BlockSpec((rows, block), lambda i: (0, i)),
            pl.BlockSpec((rows, 2 * hid), lambda i: (0, 0)),
        ],
        out_specs=[
            pl.BlockSpec((block * group, LANES), lambda i: (i, 0)),
            pl.BlockSpec((8, LANES), lambda i: (0, 0)),
        ],
        out_shape=[
            jax.ShapeDtypeStruct((d * group, LANES), BF),
            jax.ShapeDtypeStruct((8, LANES), F32),
        ],
        compiler_params=params(),
        cost_estimate=pl.CostEstimate(
            flops=4 * rows * d * hid, bytes_accessed=8 * d * hid, transcendentals=0
        ),
    )(tok, pre)
    out = out.reshape(d, tiles, 2, LANES).transpose(0, 2, 1, 3).reshape(d, 2, hid)
    return out, token


def down_kernel(hid_ref, scaled_ref, out_ref, token_ref):
    token_ref[...] = jnp.zeros_like(token_ref)
    out_ref[...] = lax.dot_general(
        hid_ref[...], scaled_ref[...], TN, preferred_element_type=F32
    ).astype(BF)


def grad_down(hidden, scaled, block=768):
    rows, d = scaled.shape
    hid = hidden.shape[1]
    return pl.pallas_call(
        down_kernel,
        grid=(d // block,),
        in_specs=[
            pl.BlockSpec((rows, hid), lambda i: (0, 0)),
            pl.BlockSpec((rows, block), lambda i: (0, i)),
        ],
        out_specs=[
            pl.BlockSpec((hid, block), lambda i: (0, i)),
            pl.BlockSpec((8, LANES), lambda i: (0, 0)),
        ],
        out_shape=[
            jax.ShapeDtypeStruct((hid, d), BF),
            jax.ShapeDtypeStruct((8, LANES), F32),
        ],
        compiler_params=params(),
        cost_estimate=pl.CostEstimate(
            flops=2 * rows * d * hid, bytes_accessed=4 * d * hid, transcendentals=0
        ),
    )(hidden, scaled)


def shards(tokens, grad_out, expert_ids, gate_probs, device_expert, w_in, w_down):
    n = lax.axis_size("dev")
    rows, width = tokens.shape
    hid = w_down.shape[0]
    ids_t = expert_ids.T
    probs_t = gate_probs.T
    bits = xor_bits(n)

    own = pl.pallas_call(
        pack_kernel,
        in_specs=[VMEM] * 4,
        out_specs=VMEM,
        out_shape=jax.ShapeDtypeStruct((rows, 2 * width + META), BF),
        compiler_params=params(60),
    )(tokens, grad_out, ids_t, probs_t)

    held = {0: own}
    order = [0]
    w_flat = split_weights(w_in)
    for step, bit in enumerate(bits):
        for o in order:
            held[o ^ bit] = xor_swap(held[o], bit)
        if bit == 2:
            last = order[1] ^ bit
            held[last], w_flat = lax.optimization_barrier((held[last], w_flat))
        order = order + [o ^ bit for o in order]

    total = n * rows
    half = total // 2
    tok, scaled, pre, hidden, gate, send = pl.pallas_call(
        functools.partial(main_kernel, n),
        in_specs=[SMEM] + [VMEM] * (n + 2),
        out_specs=[VMEM] * 6,
        out_shape=[
            jax.ShapeDtypeStruct((total, width), BF),
            jax.ShapeDtypeStruct((total, width), BF),
            jax.ShapeDtypeStruct((total, 2 * hid), BF),
            jax.ShapeDtypeStruct((total, hid), BF),
            jax.ShapeDtypeStruct((total, META), F32),
            jax.ShapeDtypeStruct((half, width + META), BF),
        ],
        scratch_shapes=[pltpu.VMEM((total, width), BF)],
        compiler_params=params(),
    )(device_expert, *[held[o] for o in order], w_flat, w_down)

    got = xor_swap(send, 1)
    mine = pl.pallas_call(
        own_kernel,
        in_specs=[SMEM] + [VMEM] * 3,
        out_specs=VMEM,
        out_shape=jax.ShapeDtypeStruct((half, width + META), F32),
        compiler_params=params(),
    )(device_expert, pre, w_flat, gate)
    grad_w_in, after_in = grad_in(tok, pre)
    grad_w_down, after_down = grad_down(hidden, scaled)
    for step, bit in enumerate(bits[-2::-1]):
        mine, send = add_step(mine, got, (gate, after_in, after_down)[min(step, 2)])
        got = xor_swap(send, bit)

    grad_tokens, gates_t = pl.pallas_call(
        last_kernel,
        in_specs=[VMEM] * 3,
        out_specs=[VMEM] * 2,
        out_shape=[
            jax.ShapeDtypeStruct((rows, width), BF),
            jax.ShapeDtypeStruct((expert_ids.shape[1], rows), F32),
        ],
        compiler_params=params(),
    )(mine, got, ids_t)
    return grad_tokens, gates_t.T, grad_w_in, grad_w_down


def solution(mesh):
    return jax.shard_map(
        shards,
        mesh=mesh,
        in_specs=(
            P(("parts", "dev"), None),
            P(("parts", "dev"), None),
            P(("parts", "dev"), None),
            P(("parts", "dev"), None),
            P(),
            P(None, None, "dev"),
            P("dev", None),
        ),
        out_specs=(
            P(("parts", "dev"), None),
            P(("parts", "dev"), None),
            P("parts", None, "dev"),
            P(("parts", "dev"), None),
        ),
        check_vma=False,
    )
```

```python
import functools

import jax
import jax.numpy as jnp
from jax import lax
from jax.experimental import pallas as pl
from jax.experimental.pallas import tpu as pltpu
from jax.sharding import PartitionSpec as P

EXP_WIN = 4
META = 128
LANES = 128
SIDE = 256
BF = jnp.bfloat16
F32 = jnp.float32
VMEM = pl.BlockSpec(memory_space=pltpu.VMEM)
ANY = pl.BlockSpec(memory_space=pl.ANY)
SMEM = pl.BlockSpec(memory_space=pltpu.SMEM)
NT = (((1,), (1,)), ((), ()))
TN = (((0,), (0,)), ((), ()))


def params(mib=16):
    return pltpu.CompilerParams(vmem_limit_bytes=mib << 20)


def xor_swap(value, bit):
    n = lax.axis_size("dev")
    other = {2: 4, 4: 2}.get(bit, bit) if n >= 8 else bit
    return lax.ppermute(value, "dev", [(i, i ^ (other if i & 1 else bit)) for i in range(n)])


def xor_bits(n):
    bits = []
    bit = n // 2
    while bit:
        bits.append(bit)
        bit //= 2
    return bits


def pack_kernel(tok_ref, grad_ref, ids_ref, prob_ref, out_ref):
    rows, width = tok_ref.shape
    out_ref[:, :width] = tok_ref[...]
    out_ref[:, width : 2 * width] = grad_ref[...]
    top = ids_ref.shape[0]
    diag = lax.broadcasted_iota(jnp.int32, (rows, rows), 0) == lax.broadcasted_iota(
        jnp.int32, (rows, rows), 1
    )
    lane = lax.broadcasted_iota(jnp.int32, (rows, META), 1)
    expert = lane % EXP_WIN
    flag = jnp.zeros((rows, META), F32)
    prob = jnp.zeros((rows, META), F32)
    for k in range(top):
        ids = jnp.broadcast_to(ids_ref[k : k + 1, :].astype(F32), (rows, rows))
        val = jnp.broadcast_to(prob_ref[k : k + 1, :], (rows, rows))
        ids = jnp.sum(jnp.where(diag, ids, 0.0), 1, keepdims=True)
        val = jnp.sum(jnp.where(diag, val, 0.0), 1, keepdims=True)
        hit = expert.astype(F32) == ids
        flag = jnp.where(hit, 1.0, flag)
        prob = prob + jnp.where(hit, val, 0.0)
    high = prob.astype(BF).astype(F32)
    mid = (prob - high).astype(BF).astype(F32)
    low = prob - high - mid
    part = lane // EXP_WIN
    meta = jnp.where(part == 0, flag, 0.0)
    meta = jnp.where(part == 1, high, meta)
    meta = jnp.where(part == 2, mid, meta)
    meta = jnp.where(part == 3, low, meta)
    out_ref[:, 2 * width :] = meta.astype(BF)


def shuffle(group, inverse=False):
    per = SIDE // group
    row = lax.broadcasted_iota(jnp.int32, (SIDE, SIDE), 0)
    col = lax.broadcasted_iota(jnp.int32, (SIDE, SIDE), 1)
    if inverse:
        row, col = col, row
    return (col == (row % per) * group + row // per).astype(BF)


def split_kernel(part, w_hbm, out_ref, w_ref, sems):
    d, wide = out_ref.shape
    group = wide // LANES
    per = SIDE // group
    tiles = group // 2
    take = shuffle(group)
    parts = sems.shape[0]
    size = d * group // parts
    copies = [
        pltpu.make_async_copy(
            w_hbm.at[pl.ds((part * parts + i) * size, size), :],
            w_ref.at[pl.ds(i * size, size), :],
            sems.at[i],
        )
        for i in range(parts)
    ]
    for copy in copies:
        copy.start()
    for s in range(0, d // per, 2):
        if s * SIDE % size == 0:
            copies[s * SIDE // size].wait()
        pair = jnp.concatenate(
            [w_ref[s * SIDE : (s + 1) * SIDE, :], w_ref[(s + 1) * SIDE : (s + 2) * SIDE, :]], 1
        )
        rows = jnp.dot(take, pair, preferred_element_type=F32).astype(BF)
        for q in range(group):
            column = (q % 2 * tiles + q // 2) * LANES
            for half in range(2):
                here = (s + half) * per
                out_ref[here : here + per, column : column + LANES] = rows[
                    q * per : (q + 1) * per, half * LANES : (half + 1) * LANES
                ]


def lane_rows(w_in):
    d, two, hid = w_in.shape
    tiles = hid // LANES
    return w_in.reshape(d, two, tiles, LANES).transpose(0, 2, 1, 3).reshape(-1, LANES)


def split_weights(view, part, d, wide):
    rows = view.shape[0] // 2
    return pl.pallas_call(
        functools.partial(split_kernel, part),
        in_specs=[ANY],
        out_specs=VMEM,
        out_shape=jax.ShapeDtypeStruct((d // 2, wide), BF),
        scratch_shapes=[pltpu.VMEM((rows, LANES), BF), pltpu.SemaphoreType.DMA((3,))],
        compiler_params=params(50),
        cost_estimate=pl.CostEstimate(
            flops=2 * rows * SIDE * LANES, bytes_accessed=4 * rows * LANES, transcendentals=0
        ),
    )(view)


def put_gate(out_ref, value, expert, width):
    rows = value.shape[0]
    lane = lax.broadcasted_iota(jnp.int32, (rows, META), 1)
    high = value.astype(BF).astype(F32)
    low = value - high
    pair = jnp.where(lane == expert, high, 0.0)
    pair = jnp.where(lane == expert + EXP_WIN, low, pair)
    out_ref[:, width:] = pair.astype(out_ref.dtype)


def main_kernel(n, owner_ref, *refs):
    pieces, refs = refs[:n], refs[n:]
    low_ref, high_ref, down_ref, tok_ref, grad_ref, pre_ref, hid_ref, prob_ref, own_ref, send_ref = refs
    rows = pieces[0].shape[0]
    width = down_ref.shape[1]
    hid = down_ref.shape[0]
    cut = low_ref.shape[0]
    expert = owner_ref[lax.axis_index("dev")]
    metas = []
    for i in range(0, n, 2):
        pair = [pieces[i][...].astype(F32), pieces[i + 1][...].astype(F32)]
        both = jnp.concatenate(pair, 0)
        here = pl.ds(i * rows, 2 * rows)
        tok_ref[here, :] = both[:, :width].astype(BF)
        grad_ref[here, :] = both[:, width : 2 * width].astype(BF)
        metas.append(both[:, 2 * width :])
    meta = jnp.concatenate(metas, 0)
    lane = lax.broadcasted_iota(jnp.int32, meta.shape, 1)
    routed = jnp.sum(jnp.where(lane == expert, meta, 0.0), 1, keepdims=True)
    prob = jnp.sum(
        jnp.where((lane >= EXP_WIN) & (lane % EXP_WIN == expert), meta, 0.0), 1, keepdims=True
    )
    prob_ref[...] = jnp.broadcast_to(prob, prob_ref.shape)
    projected = jnp.dot(tok_ref[:, :cut], low_ref[...], preferred_element_type=F32)
    projected += jnp.dot(tok_ref[:, cut:], high_ref[...], preferred_element_type=F32)
    gate, up = projected[:, :hid], projected[:, hid:]
    back = lax.dot_general(grad_ref[...], down_ref[...], NT, preferred_element_type=F32)
    logistic = jax.nn.sigmoid(gate)
    activated = gate * logistic
    hidden = (activated * up).astype(BF)
    hid_ref[...] = hidden
    gate_sum = routed * jnp.sum(hidden.astype(F32) * back, 1, keepdims=True)
    hidden_grad = prob * back
    pre_gate = hidden_grad * up * logistic * (1.0 + gate * (1.0 - logistic))
    pre_ref[:, :hid] = pre_gate.astype(BF)
    pre_ref[:, hid:] = (hidden_grad * activated).astype(BF)
    half = n * rows // 2
    put_gate(own_ref, gate_sum[:half], expert, width)
    put_gate(send_ref, gate_sum[half:], expert, width)
    step = cut // 2
    for c in range(0, width, step):
        weights = low_ref if c < cut else high_ref
        start = c if c < cut else c - cut
        part = lax.dot_general(
            pre_ref[...], weights[start : start + step, :], NT, preferred_element_type=F32
        )
        own_ref[:, c : c + step] = part[:half]
        send_ref[:, c : c + step] = part[half:].astype(BF)


def add_kernel(parts, own_ref, *refs):
    got, (keep_ref, *send_refs) = refs[: -parts - 1], refs[-parts:]
    total = own_ref[...]
    for got_ref in got:
        total += got_ref[...].astype(F32)
    rows = keep_ref.shape[0]
    width = total.shape[1] - META
    keep_ref[...] = total[:rows]
    for i, send_ref in enumerate(send_refs, 1):
        here = total[i * rows : (i + 1) * rows]
        send_ref[:, :width] = here[:, :width].astype(BF)
        tail = here[:, width:]
        lane = lax.broadcasted_iota(jnp.int32, tail.shape, 1)
        value = tail + pltpu.roll(tail, META - EXP_WIN, 1)
        high = value.astype(BF).astype(F32)
        low = pltpu.roll(value - high, EXP_WIN, 1)
        pair = jnp.where(lane < EXP_WIN, high, jnp.where(lane < 2 * EXP_WIN, low, 0.0))
        send_ref[:, width:] = pair.astype(BF)


def add_step(own, got, after, parts):
    rows, width = own.shape
    part = rows // parts
    keep, *send = pl.pallas_call(
        functools.partial(add_kernel, parts),
        in_specs=[VMEM] * (1 + len(got)) + [ANY],
        out_specs=[VMEM] * parts,
        out_shape=[jax.ShapeDtypeStruct((part, width), F32)]
        + [jax.ShapeDtypeStruct((part, width), BF)] * (parts - 1),
        compiler_params=params(),
        cost_estimate=pl.CostEstimate(
            flops=rows * width, bytes_accessed=8 * rows * width, transcendentals=0
        ),
    )(own, *got, after)
    return keep, send


def last_kernel(own_ref, got_ref, ids_ref, after_ref, tok_ref, gates_ref):
    total = own_ref[...] + got_ref[...].astype(F32)
    rows = total.shape[0]
    width = total.shape[1] - META
    tok_ref[...] = total[:, :width].astype(BF)
    tail = total[:, width:]
    value = tail + pltpu.roll(tail, META - EXP_WIN, 1)
    lane = lax.broadcasted_iota(jnp.int32, (rows, META), 1)
    diag = lax.broadcasted_iota(jnp.int32, (rows, rows), 0) == lax.broadcasted_iota(
        jnp.int32, (rows, rows), 1
    )
    for k in range(ids_ref.shape[0]):
        ids = jnp.broadcast_to(ids_ref[k : k + 1, :].astype(F32), (rows, rows))
        ids = jnp.sum(jnp.where(diag, ids, 0.0), 1, keepdims=True)
        hit = (lane.astype(F32) == ids) & (lane < EXP_WIN)
        column = jnp.sum(jnp.where(hit, value, 0.0), 1, keepdims=True)
        square = jnp.where(diag, jnp.broadcast_to(column, (rows, rows)), 0.0)
        gates_ref[k : k + 1, :] = jnp.sum(square, 0, keepdims=True)


def win_kernel(tok_ref, pre_ref, out_ref, token_ref):
    wide = pre_ref.shape[1]
    group = wide // LANES
    per = SIDE // group
    tiles = group // 2
    put = shuffle(group, inverse=True)
    block = lax.dot_general(
        tok_ref[...], pre_ref[...], TN, preferred_element_type=F32
    ).astype(BF)
    for s in range(0, tok_ref.shape[1] // per, 2):
        sides = []
        for half in range(2):
            here = (s + half) * per
            sides.append(
                jnp.concatenate(
                    [
                        block[here : here + per, c * LANES : (c + 1) * LANES]
                        for c in [q % 2 * tiles + q // 2 for q in range(group)]
                    ],
                    0,
                )
            )
        rows = jnp.dot(put, jnp.concatenate(sides, 1), preferred_element_type=F32).astype(BF)
        out_ref[s * SIDE : (s + 1) * SIDE, :] = rows[:, :LANES]
        out_ref[(s + 1) * SIDE : (s + 2) * SIDE, :] = rows[:, LANES:]
    token_ref[...] = jnp.zeros_like(token_ref)


def grad_in(tok, pre, after, first, count, out=None, block=512):
    rows, d = tok.shape
    wide = pre.shape[1]
    group = wide // LANES
    kernel = lambda t, p, *refs: win_kernel(t, p, refs[-2], refs[-1])
    return pl.pallas_call(
        kernel,
        grid=(count,),
        in_specs=[
            pl.BlockSpec((rows, block), lambda i: (0, i + first)),
            pl.BlockSpec((rows, wide), lambda i: (0, 0)),
            ANY,
        ]
        + ([] if out is None else [ANY]),
        out_specs=[
            pl.BlockSpec((block * group, LANES), lambda i: (i + first, 0)),
            pl.BlockSpec((8, LANES), lambda i: (0, 0)),
        ],
        out_shape=[
            jax.ShapeDtypeStruct((d * group, LANES), BF),
            jax.ShapeDtypeStruct((8, LANES), F32),
        ],
        input_output_aliases={} if out is None else {3: 0},
        compiler_params=params(),
        cost_estimate=pl.CostEstimate(
            flops=2 * rows * count * block * wide,
            bytes_accessed=4 * count * block * wide,
            transcendentals=0,
        ),
    )(tok, pre, after, *([] if out is None else [out]))


def down_kernel(hid_ref, grad_ref, prob_ref, after_ref, out_ref, token_ref):
    token_ref[...] = jnp.zeros_like(token_ref)
    scaled = (prob_ref[:, :1] * grad_ref[...].astype(F32)).astype(BF)
    out_ref[...] = lax.dot_general(
        hid_ref[...], scaled, TN, preferred_element_type=F32
    ).astype(BF)


def grad_down(hidden, grads, prob, after, block=768):
    rows, d = grads.shape
    hid = hidden.shape[1]
    return pl.pallas_call(
        down_kernel,
        grid=(d // block,),
        in_specs=[
            pl.BlockSpec((rows, hid), lambda i: (0, 0)),
            pl.BlockSpec((rows, block), lambda i: (0, i)),
            pl.BlockSpec((rows, META), lambda i: (0, 0)),
            ANY,
        ],
        out_specs=[
            pl.BlockSpec((hid, block), lambda i: (0, i)),
            pl.BlockSpec((8, LANES), lambda i: (0, 0)),
        ],
        out_shape=[
            jax.ShapeDtypeStruct((hid, d), BF),
            jax.ShapeDtypeStruct((8, LANES), F32),
        ],
        compiler_params=params(),
        cost_estimate=pl.CostEstimate(
            flops=2 * rows * d * hid, bytes_accessed=4 * d * hid, transcendentals=0
        ),
    )(hidden, grads, prob, after)


def shards(tokens, grad_out, expert_ids, gate_probs, device_expert, w_in, w_down):
    n = lax.axis_size("dev")
    rows, width = tokens.shape
    hid = w_down.shape[0]
    ids_t = expert_ids.T
    probs_t = gate_probs.T
    bits = xor_bits(n)

    own = pl.pallas_call(
        pack_kernel,
        in_specs=[VMEM] * 4,
        out_specs=VMEM,
        out_shape=jax.ShapeDtypeStruct((rows, 2 * width + META), BF),
        compiler_params=params(60),
    )(tokens, grad_out, ids_t, probs_t)

    order = [0]
    for bit in bits:
        order = order + [o ^ bit for o in order]
    view = lane_rows(w_in)
    held = {0: own}
    far, near = n // 2, n // 4
    cross = near + 2

    def piece(o):
        if o not in held:
            bit = near if o == cross else o & -o
            held[o] = xor_swap(piece(o ^ bit), bit)
        return held[o]

    weights = []
    for part, o in enumerate((far, far + near)):
        half_split = split_weights(view, part, width, 2 * hid)
        held[o], half_split = lax.optimization_barrier((piece(o), half_split))
        weights.append(half_split)
    for o in order:
        piece(o)

    total = n * rows
    half = total // 2
    tok, grads, pre, hidden, prob, mine, send = pl.pallas_call(
        functools.partial(main_kernel, n),
        in_specs=[SMEM] + [VMEM] * (n + 3),
        out_specs=[VMEM] * 7,
        out_shape=[
            jax.ShapeDtypeStruct((total, width), BF),
            jax.ShapeDtypeStruct((total, width), BF),
            jax.ShapeDtypeStruct((total, 2 * hid), BF),
            jax.ShapeDtypeStruct((total, hid), BF),
            jax.ShapeDtypeStruct((total, META), F32),
            jax.ShapeDtypeStruct((half, width + META), F32),
            jax.ShapeDtypeStruct((half, width + META), BF),
        ],
        compiler_params=params(),
    )(device_expert, *[held[o] for o in order], *weights, w_down)

    steps = width // 512
    first = 2
    got = [xor_swap(send, 1)]
    grad_w_in, after = grad_in(tok, pre, prob, 0, first)
    mine, (by_near, by_side, by_both) = add_step(mine, got, after, 4)
    got = [xor_swap(by_both, 6), xor_swap(by_side, 2), xor_swap(by_near, 4)]
    grad_w_down, after = grad_down(hidden, grads, prob, mine)
    for bit in bits[-4::-1]:
        mine, (send,) = add_step(mine, got, after, 2)
        got = [xor_swap(send, bit)]
        if bit == 8:
            grad_w_in, after = grad_in(tok, pre, mine, first, steps - first, grad_w_in)
    tiles = hid // LANES
    grad_w_in = grad_w_in.reshape(width, tiles, 2, LANES).transpose(0, 2, 1, 3)
    grad_w_in = grad_w_in.reshape(width, 2, hid)
    grad_tokens, gates_t = pl.pallas_call(
        last_kernel,
        in_specs=[VMEM] * 3 + [ANY],
        out_specs=[VMEM] * 2,
        out_shape=[
            jax.ShapeDtypeStruct((rows, width), BF),
            jax.ShapeDtypeStruct((expert_ids.shape[1], rows), F32),
        ],
        compiler_params=params(),
    )(mine, *got, ids_t, after)
    return grad_tokens, gates_t.T, grad_w_in, grad_w_down


def solution(mesh):
    return jax.shard_map(
        shards,
        mesh=mesh,
        in_specs=(
            P(("parts", "dev"), None),
            P(("parts", "dev"), None),
            P(("parts", "dev"), None),
            P(("parts", "dev"), None),
            P(),
            P(None, None, "dev"),
            P("dev", None),
        ),
        out_specs=(
            P(("parts", "dev"), None),
            P(("parts", "dev"), None),
            P("parts", None, "dev"),
            P(("parts", "dev"), None),
        ),
        check_vma=False,
    )
```

```python
import functools

import jax
import jax.numpy as jnp
from jax import lax
from jax.experimental import pallas as pl
from jax.experimental.pallas import tpu as pltpu
from jax.sharding import PartitionSpec as P

EXP_WIN = 4
META = 128
LANES = 128
SIDE = 256
BF = jnp.bfloat16
F32 = jnp.float32
VMEM = pl.BlockSpec(memory_space=pltpu.VMEM)
ANY = pl.BlockSpec(memory_space=pl.ANY)
SMEM = pl.BlockSpec(memory_space=pltpu.SMEM)
NT = (((1,), (1,)), ((), ()))
TN = (((0,), (0,)), ((), ()))


def params(mib=16):
    return pltpu.CompilerParams(vmem_limit_bytes=mib << 20)


def xor_swap(value, bit):
    n = lax.axis_size("dev")
    other = {2: 4, 4: 2}.get(bit, bit) if n >= 8 else bit
    return lax.ppermute(value, "dev", [(i, i ^ (other if i & 1 else bit)) for i in range(n)])


def xor_bits(n):
    bits = []
    bit = n // 2
    while bit:
        bits.append(bit)
        bit //= 2
    return bits


def pack_kernel(tok_ref, grad_ref, ids_ref, prob_ref, out_ref):
    rows, width = tok_ref.shape
    out_ref[:, :width] = tok_ref[...]
    out_ref[:, width : 2 * width] = grad_ref[...]
    top = ids_ref.shape[0]
    diag = lax.broadcasted_iota(jnp.int32, (rows, rows), 0) == lax.broadcasted_iota(
        jnp.int32, (rows, rows), 1
    )
    lane = lax.broadcasted_iota(jnp.int32, (rows, META), 1)
    expert = lane % EXP_WIN
    flag = jnp.zeros((rows, META), F32)
    prob = jnp.zeros((rows, META), F32)
    for k in range(top):
        ids = jnp.broadcast_to(ids_ref[k : k + 1, :].astype(F32), (rows, rows))
        val = jnp.broadcast_to(prob_ref[k : k + 1, :], (rows, rows))
        ids = jnp.sum(jnp.where(diag, ids, 0.0), 1, keepdims=True)
        val = jnp.sum(jnp.where(diag, val, 0.0), 1, keepdims=True)
        hit = expert.astype(F32) == ids
        flag = jnp.where(hit, 1.0, flag)
        prob = prob + jnp.where(hit, val, 0.0)
    high = prob.astype(BF).astype(F32)
    mid = (prob - high).astype(BF).astype(F32)
    low = prob - high - mid
    part = lane // EXP_WIN
    meta = jnp.where(part == 0, flag, 0.0)
    meta = jnp.where(part == 1, high, meta)
    meta = jnp.where(part == 2, mid, meta)
    meta = jnp.where(part == 3, low, meta)
    out_ref[:, 2 * width :] = meta.astype(BF)


def shuffle(group, inverse=False):
    per = SIDE // group
    row = lax.broadcasted_iota(jnp.int32, (SIDE, SIDE), 0)
    col = lax.broadcasted_iota(jnp.int32, (SIDE, SIDE), 1)
    if inverse:
        row, col = col, row
    return (col == (row % per) * group + row // per).astype(BF)


def split_rows(part, w_hbm, out_ref, w_ref, sems):
    d, wide = out_ref.shape
    group = wide // LANES
    per = SIDE // group
    tiles = group // 2
    take = shuffle(group)
    parts = sems.shape[0]
    size = d * group // parts
    copies = [
        pltpu.make_async_copy(
            w_hbm.at[pl.ds((part * parts + i) * size, size), :],
            w_ref.at[pl.ds(i * size, size), :],
            sems.at[i],
        )
        for i in range(parts)
    ]
    for copy in copies:
        copy.start()
    for s in range(0, d // per, 2):
        if s * SIDE % size == 0:
            copies[s * SIDE // size].wait()
        pair = jnp.concatenate(
            [w_ref[s * SIDE : (s + 1) * SIDE, :], w_ref[(s + 1) * SIDE : (s + 2) * SIDE, :]], 1
        )
        rows = jnp.dot(take, pair, preferred_element_type=F32).astype(BF)
        for q in range(group):
            column = (q % 2 * tiles + q // 2) * LANES
            for half in range(2):
                here = (s + half) * per
                out_ref[here : here + per, column : column + LANES] = rows[
                    q * per : (q + 1) * per, half * LANES : (half + 1) * LANES
                ]


def split_kernel(part, when, w_hbm, *refs):
    done_ref, (out_ref, w_ref, sems) = refs[:-3], refs[-3:]
    if when is None:
        split_rows(part, w_hbm, out_ref, w_ref, sems)
        return
    mine = lax.axis_index("dev") % 2 == when

    @pl.when(mine)
    def _():
        split_rows(part, w_hbm, out_ref, w_ref, sems)

    if done_ref:

        @pl.when(jnp.logical_not(mine))
        def _():
            out_ref[...] = done_ref[0][...]


def lane_rows(w_in):
    d, two, hid = w_in.shape
    tiles = hid // LANES
    return w_in.reshape(d, two, tiles, LANES).transpose(0, 2, 1, 3).reshape(-1, LANES)


def split_weights(view, part, d, wide, when=None, *done):
    rows = view.shape[0] // 2
    return pl.pallas_call(
        functools.partial(split_kernel, part, when),
        in_specs=[ANY] + [VMEM] * len(done),
        out_specs=VMEM,
        out_shape=jax.ShapeDtypeStruct((d // 2, wide), BF),
        scratch_shapes=[pltpu.VMEM((rows, LANES), BF), pltpu.SemaphoreType.DMA((3,))],
        compiler_params=params(50),
        cost_estimate=pl.CostEstimate(
            flops=2 * rows * SIDE * LANES, bytes_accessed=4 * rows * LANES, transcendentals=0
        ),
    )(view, *done)


def put_gate(out_ref, value, expert, width):
    rows = value.shape[0]
    lane = lax.broadcasted_iota(jnp.int32, (rows, META), 1)
    high = value.astype(BF).astype(F32)
    low = value - high
    pair = jnp.where(lane == expert, high, 0.0)
    pair = jnp.where(lane == expert + EXP_WIN, low, pair)
    out_ref[:, width:] = pair.astype(out_ref.dtype)


def main_kernel(n, owner_ref, *refs):
    pieces, refs = refs[:n], refs[n:]
    low_ref, high_ref, down_ref, tok_ref, grad_ref, pre_ref, hid_ref, prob_ref, own_ref, send_ref = refs
    rows = pieces[0].shape[0]
    width = down_ref.shape[1]
    hid = down_ref.shape[0]
    cut = low_ref.shape[0]
    expert = owner_ref[lax.axis_index("dev")]
    metas = []
    for i in range(0, n, 2):
        pair = [pieces[i][...].astype(F32), pieces[i + 1][...].astype(F32)]
        both = jnp.concatenate(pair, 0)
        here = pl.ds(i * rows, 2 * rows)
        tok_ref[here, :] = both[:, :width].astype(BF)
        grad_ref[here, :] = both[:, width : 2 * width].astype(BF)
        metas.append(both[:, 2 * width :])
    meta = jnp.concatenate(metas, 0)
    lane = lax.broadcasted_iota(jnp.int32, meta.shape, 1)
    routed = jnp.sum(jnp.where(lane == expert, meta, 0.0), 1, keepdims=True)
    prob = jnp.sum(
        jnp.where((lane >= EXP_WIN) & (lane % EXP_WIN == expert), meta, 0.0), 1, keepdims=True
    )
    prob_ref[...] = jnp.broadcast_to(prob, prob_ref.shape)
    projected = jnp.dot(tok_ref[:, :cut], low_ref[...], preferred_element_type=F32)
    projected += jnp.dot(tok_ref[:, cut:], high_ref[...], preferred_element_type=F32)
    gate, up = projected[:, :hid], projected[:, hid:]
    back = lax.dot_general(grad_ref[...], down_ref[...], NT, preferred_element_type=F32)
    logistic = jax.nn.sigmoid(gate)
    activated = gate * logistic
    hidden = (activated * up).astype(BF)
    hid_ref[...] = hidden
    gate_sum = routed * jnp.sum(hidden.astype(F32) * back, 1, keepdims=True)
    hidden_grad = prob * back
    pre_gate = hidden_grad * up * logistic * (1.0 + gate * (1.0 - logistic))
    pre_ref[:, :hid] = pre_gate.astype(BF)
    pre_ref[:, hid:] = (hidden_grad * activated).astype(BF)
    half = n * rows // 2
    put_gate(own_ref, gate_sum[:half], expert, width)
    put_gate(send_ref, gate_sum[half:], expert, width)
    step = cut // 2
    for c in range(0, width, step):
        weights = low_ref if c < cut else high_ref
        start = c if c < cut else c - cut
        part = lax.dot_general(
            pre_ref[...], weights[start : start + step, :], NT, preferred_element_type=F32
        )
        own_ref[:, c : c + step] = part[:half]
        send_ref[:, c : c + step] = part[half:].astype(BF)


def add_kernel(parts, own_ref, *refs):
    got, (keep_ref, *send_refs) = refs[: -parts - 1], refs[-parts:]
    total = own_ref[...]
    for got_ref in got:
        total += got_ref[...].astype(F32)
    rows = keep_ref.shape[0]
    width = total.shape[1] - META
    keep_ref[...] = total[:rows]
    for i, send_ref in enumerate(send_refs, 1):
        here = total[i * rows : (i + 1) * rows]
        send_ref[:, :width] = here[:, :width].astype(BF)
        tail = here[:, width:]
        lane = lax.broadcasted_iota(jnp.int32, tail.shape, 1)
        value = tail + pltpu.roll(tail, META - EXP_WIN, 1)
        high = value.astype(BF).astype(F32)
        low = pltpu.roll(value - high, EXP_WIN, 1)
        pair = jnp.where(lane < EXP_WIN, high, jnp.where(lane < 2 * EXP_WIN, low, 0.0))
        send_ref[:, width:] = pair.astype(BF)


def add_step(own, got, after, parts):
    rows, width = own.shape
    part = rows // parts
    keep, *send = pl.pallas_call(
        functools.partial(add_kernel, parts),
        in_specs=[VMEM] * (1 + len(got)) + [ANY],
        out_specs=[VMEM] * parts,
        out_shape=[jax.ShapeDtypeStruct((part, width), F32)]
        + [jax.ShapeDtypeStruct((part, width), BF)] * (parts - 1),
        compiler_params=params(),
        cost_estimate=pl.CostEstimate(
            flops=rows * width, bytes_accessed=8 * rows * width, transcendentals=0
        ),
    )(own, *got, after)
    return keep, send


def last_kernel(own_ref, got_ref, ids_ref, after_ref, tok_ref, gates_ref):
    total = own_ref[...] + got_ref[...].astype(F32)
    rows = total.shape[0]
    width = total.shape[1] - META
    tok_ref[...] = total[:, :width].astype(BF)
    tail = total[:, width:]
    value = tail + pltpu.roll(tail, META - EXP_WIN, 1)
    lane = lax.broadcasted_iota(jnp.int32, (rows, META), 1)
    diag = lax.broadcasted_iota(jnp.int32, (rows, rows), 0) == lax.broadcasted_iota(
        jnp.int32, (rows, rows), 1
    )
    for k in range(ids_ref.shape[0]):
        ids = jnp.broadcast_to(ids_ref[k : k + 1, :].astype(F32), (rows, rows))
        ids = jnp.sum(jnp.where(diag, ids, 0.0), 1, keepdims=True)
        hit = (lane.astype(F32) == ids) & (lane < EXP_WIN)
        column = jnp.sum(jnp.where(hit, value, 0.0), 1, keepdims=True)
        square = jnp.where(diag, jnp.broadcast_to(column, (rows, rows)), 0.0)
        gates_ref[k : k + 1, :] = jnp.sum(square, 0, keepdims=True)


def win_kernel(tok_ref, pre_ref, out_ref, token_ref):
    wide = pre_ref.shape[1]
    group = wide // LANES
    per = SIDE // group
    tiles = group // 2
    put = shuffle(group, inverse=True)
    block = lax.dot_general(
        tok_ref[...], pre_ref[...], TN, preferred_element_type=F32
    ).astype(BF)
    for s in range(0, tok_ref.shape[1] // per, 2):
        sides = []
        for half in range(2):
            here = (s + half) * per
            sides.append(
                jnp.concatenate(
                    [
                        block[here : here + per, c * LANES : (c + 1) * LANES]
                        for c in [q % 2 * tiles + q // 2 for q in range(group)]
                    ],
                    0,
                )
            )
        rows = jnp.dot(put, jnp.concatenate(sides, 1), preferred_element_type=F32).astype(BF)
        out_ref[s * SIDE : (s + 1) * SIDE, :] = rows[:, :LANES]
        out_ref[(s + 1) * SIDE : (s + 2) * SIDE, :] = rows[:, LANES:]
    token_ref[...] = jnp.zeros_like(token_ref)


def grad_in(tok, pre, after, first, count, out=None, block=512):
    rows, d = tok.shape
    wide = pre.shape[1]
    group = wide // LANES
    kernel = lambda t, p, *refs: win_kernel(t, p, refs[-2], refs[-1])
    return pl.pallas_call(
        kernel,
        grid=(count,),
        in_specs=[
            pl.BlockSpec((rows, block), lambda i: (0, i + first)),
            pl.BlockSpec((rows, wide), lambda i: (0, 0)),
            ANY,
        ]
        + ([] if out is None else [ANY]),
        out_specs=[
            pl.BlockSpec((block * group, LANES), lambda i: (i + first, 0)),
            pl.BlockSpec((8, LANES), lambda i: (0, 0)),
        ],
        out_shape=[
            jax.ShapeDtypeStruct((d * group, LANES), BF),
            jax.ShapeDtypeStruct((8, LANES), F32),
        ],
        input_output_aliases={} if out is None else {3: 0},
        compiler_params=params(),
        cost_estimate=pl.CostEstimate(
            flops=2 * rows * count * block * wide,
            bytes_accessed=4 * count * block * wide,
            transcendentals=0,
        ),
    )(tok, pre, after, *([] if out is None else [out]))


def down_kernel(hid_ref, grad_ref, prob_ref, after_ref, out_ref, token_ref):
    token_ref[...] = jnp.zeros_like(token_ref)
    scaled = (prob_ref[:, :1] * grad_ref[...].astype(F32)).astype(BF)
    out_ref[...] = lax.dot_general(
        hid_ref[...], scaled, TN, preferred_element_type=F32
    ).astype(BF)


def grad_down(hidden, grads, prob, after, block=768):
    rows, d = grads.shape
    hid = hidden.shape[1]
    return pl.pallas_call(
        down_kernel,
        grid=(d // block,),
        in_specs=[
            pl.BlockSpec((rows, hid), lambda i: (0, 0)),
            pl.BlockSpec((rows, block), lambda i: (0, i)),
            pl.BlockSpec((rows, META), lambda i: (0, 0)),
            ANY,
        ],
        out_specs=[
            pl.BlockSpec((hid, block), lambda i: (0, i)),
            pl.BlockSpec((8, LANES), lambda i: (0, 0)),
        ],
        out_shape=[
            jax.ShapeDtypeStruct((hid, d), BF),
            jax.ShapeDtypeStruct((8, LANES), F32),
        ],
        compiler_params=params(),
        cost_estimate=pl.CostEstimate(
            flops=2 * rows * d * hid, bytes_accessed=4 * d * hid, transcendentals=0
        ),
    )(hidden, grads, prob, after)


def shards(tokens, grad_out, expert_ids, gate_probs, device_expert, w_in, w_down):
    n = lax.axis_size("dev")
    rows, width = tokens.shape
    hid = w_down.shape[0]
    ids_t = expert_ids.T
    probs_t = gate_probs.T
    bits = xor_bits(n)

    own = pl.pallas_call(
        pack_kernel,
        in_specs=[VMEM] * 4,
        out_specs=VMEM,
        out_shape=jax.ShapeDtypeStruct((rows, 2 * width + META), BF),
        compiler_params=params(60),
    )(tokens, grad_out, ids_t, probs_t)

    order = [0]
    for bit in bits:
        order = order + [o ^ bit for o in order]
    view = lane_rows(w_in)
    held = {0: own}
    far, near = n // 2, n // 4
    cross = near + 2

    def piece(o):
        if o not in held:
            bit = near if o == cross else o & -o
            held[o] = xor_swap(piece(o ^ bit), bit)
        return held[o]

    early = split_weights(view, 0, width, 2 * hid, 1)
    held[0], early = lax.optimization_barrier((own, early))
    low = split_weights(view, 0, width, 2 * hid, 0, early)
    high = split_weights(view, 1, width, 2 * hid)
    held[far], low = lax.optimization_barrier((piece(far), low))
    held[far + 2], high = lax.optimization_barrier((piece(far + 2), high))
    weights = [low, high]
    for o in order:
        piece(o)

    total = n * rows
    half = total // 2
    tok, grads, pre, hidden, prob, mine, send = pl.pallas_call(
        functools.partial(main_kernel, n),
        in_specs=[SMEM] + [VMEM] * (n + 3),
        out_specs=[VMEM] * 7,
        out_shape=[
            jax.ShapeDtypeStruct((total, width), BF),
            jax.ShapeDtypeStruct((total, width), BF),
            jax.ShapeDtypeStruct((total, 2 * hid), BF),
            jax.ShapeDtypeStruct((total, hid), BF),
            jax.ShapeDtypeStruct((total, META), F32),
            jax.ShapeDtypeStruct((half, width + META), F32),
            jax.ShapeDtypeStruct((half, width + META), BF),
        ],
        compiler_params=params(),
    )(device_expert, *[held[o] for o in order], *weights, w_down)

    steps = width // 512
    got = [xor_swap(send, 1)]
    grad_w_in, after = grad_in(tok, pre, prob, 0, 1)
    mine, (by_near, by_side, by_both) = add_step(mine, got, after, 4)
    got = [xor_swap(by_both, 6), xor_swap(by_side, 2), xor_swap(by_near, 4)]
    grad_w_in, after = grad_in(tok, pre, mine, 1, 2, grad_w_in)
    grad_w_down, after = grad_down(hidden, grads, prob, after)
    for bit in bits[-4::-1]:
        mine, (send,) = add_step(mine, got, after, 2)
        got = [xor_swap(send, bit)]
        if bit == 8:
            grad_w_in, after = grad_in(tok, pre, mine, 3, steps - 3, grad_w_in)
    tiles = hid // LANES
    grad_w_in = grad_w_in.reshape(width, tiles, 2, LANES).transpose(0, 2, 1, 3)
    grad_w_in = grad_w_in.reshape(width, 2, hid)
    grad_tokens, gates_t = pl.pallas_call(
        last_kernel,
        in_specs=[VMEM] * 3 + [ANY],
        out_specs=[VMEM] * 2,
        out_shape=[
            jax.ShapeDtypeStruct((rows, width), BF),
            jax.ShapeDtypeStruct((expert_ids.shape[1], rows), F32),
        ],
        compiler_params=params(),
    )(mine, *got, ids_t, after)
    return grad_tokens, gates_t.T, grad_w_in, grad_w_down


def solution(mesh):
    return jax.shard_map(
        shards,
        mesh=mesh,
        in_specs=(
            P(("parts", "dev"), None),
            P(("parts", "dev"), None),
            P(("parts", "dev"), None),
            P(("parts", "dev"), None),
            P(),
            P(None, None, "dev"),
            P("dev", None),
        ),
        out_specs=(
            P(("parts", "dev"), None),
            P(("parts", "dev"), None),
            P("parts", None, "dev"),
            P(("parts", "dev"), None),
        ),
        check_vma=False,
    )
```

```python
import functools

import jax
import jax.numpy as jnp
from jax import lax
from jax.experimental import pallas as pl
from jax.experimental.pallas import tpu as pltpu
from jax.sharding import PartitionSpec as P

EXP_WIN = 4
META = 128
LANES = 128
SIDE = 256
BF = jnp.bfloat16
F32 = jnp.float32
VMEM = pl.BlockSpec(memory_space=pltpu.VMEM)
ANY = pl.BlockSpec(memory_space=pl.ANY)
SMEM = pl.BlockSpec(memory_space=pltpu.SMEM)
NT = (((1,), (1,)), ((), ()))
TN = (((0,), (0,)), ((), ()))


def params(mib=16):
    return pltpu.CompilerParams(vmem_limit_bytes=mib << 20)


def xor_swap(value, bit):
    n = lax.axis_size("dev")
    other = {2: 4, 4: 2}.get(bit, bit) if n >= 8 else bit
    return lax.ppermute(value, "dev", [(i, i ^ (other if i & 1 else bit)) for i in range(n)])


def xor_bits(n):
    bits = []
    bit = n // 2
    while bit:
        bits.append(bit)
        bit //= 2
    return bits


def pack_kernel(tok_ref, grad_ref, ids_ref, prob_ref, out_ref):
    rows, width = tok_ref.shape
    out_ref[:, :width] = tok_ref[...]
    out_ref[:, width : 2 * width] = grad_ref[...]
    top = ids_ref.shape[0]
    diag = lax.broadcasted_iota(jnp.int32, (rows, rows), 0) == lax.broadcasted_iota(
        jnp.int32, (rows, rows), 1
    )
    lane = lax.broadcasted_iota(jnp.int32, (rows, META), 1)
    expert = lane % EXP_WIN
    flag = jnp.zeros((rows, META), F32)
    prob = jnp.zeros((rows, META), F32)
    for k in range(top):
        ids = jnp.broadcast_to(ids_ref[k : k + 1, :].astype(F32), (rows, rows))
        val = jnp.broadcast_to(prob_ref[k : k + 1, :], (rows, rows))
        ids = jnp.sum(jnp.where(diag, ids, 0.0), 1, keepdims=True)
        val = jnp.sum(jnp.where(diag, val, 0.0), 1, keepdims=True)
        hit = expert.astype(F32) == ids
        flag = jnp.where(hit, 1.0, flag)
        prob = prob + jnp.where(hit, val, 0.0)
    high = prob.astype(BF).astype(F32)
    mid = (prob - high).astype(BF).astype(F32)
    low = prob - high - mid
    part = lane // EXP_WIN
    meta = jnp.where(part == 0, flag, 0.0)
    meta = jnp.where(part == 1, high, meta)
    meta = jnp.where(part == 2, mid, meta)
    meta = jnp.where(part == 3, low, meta)
    out_ref[:, 2 * width :] = meta.astype(BF)


def shuffle(group, inverse=False):
    per = SIDE // group
    row = lax.broadcasted_iota(jnp.int32, (SIDE, SIDE), 0)
    col = lax.broadcasted_iota(jnp.int32, (SIDE, SIDE), 1)
    if inverse:
        row, col = col, row
    return (col == (row % per) * group + row // per).astype(BF)


def split_rows(part, w_hbm, out_ref, w_ref, sems):
    d, wide = out_ref.shape
    group = wide // LANES
    per = SIDE // group
    tiles = group // 2
    take = shuffle(group)
    parts = sems.shape[0]
    size = d * group // parts
    copies = [
        pltpu.make_async_copy(
            w_hbm.at[pl.ds((part * parts + i) * size, size), :],
            w_ref.at[pl.ds(i * size, size), :],
            sems.at[i],
        )
        for i in range(parts)
    ]
    for copy in copies:
        copy.start()
    for s in range(0, d // per, 2):
        if s * SIDE % size == 0:
            copies[s * SIDE // size].wait()
        pair = jnp.concatenate(
            [w_ref[s * SIDE : (s + 1) * SIDE, :], w_ref[(s + 1) * SIDE : (s + 2) * SIDE, :]], 1
        )
        rows = jnp.dot(take, pair, preferred_element_type=F32).astype(BF)
        for q in range(group):
            column = (q % 2 * tiles + q // 2) * LANES
            for half in range(2):
                here = (s + half) * per
                out_ref[here : here + per, column : column + LANES] = rows[
                    q * per : (q + 1) * per, half * LANES : (half + 1) * LANES
                ]


def split_kernel(part, when, w_hbm, *refs):
    done_ref, (out_ref, w_ref, sems) = refs[:-3], refs[-3:]
    if when is None:
        split_rows(part, w_hbm, out_ref, w_ref, sems)
        return
    mine = lax.axis_index("dev") % 2 == when

    @pl.when(mine)
    def _():
        split_rows(part, w_hbm, out_ref, w_ref, sems)

    if done_ref:

        @pl.when(jnp.logical_not(mine))
        def _():
            out_ref[...] = done_ref[0][...]


def lane_rows(w_in):
    d, two, hid = w_in.shape
    tiles = hid // LANES
    return w_in.reshape(d, two, tiles, LANES).transpose(0, 2, 1, 3).reshape(-1, LANES)


def split_weights(view, part, d, wide, when=None, *done):
    rows = view.shape[0] // 2
    return pl.pallas_call(
        functools.partial(split_kernel, part, when),
        in_specs=[ANY] + [VMEM] * len(done),
        out_specs=VMEM,
        out_shape=jax.ShapeDtypeStruct((d // 2, wide), BF),
        scratch_shapes=[pltpu.VMEM((rows, LANES), BF), pltpu.SemaphoreType.DMA((3,))],
        compiler_params=params(50),
        cost_estimate=pl.CostEstimate(
            flops=2 * rows * SIDE * LANES, bytes_accessed=4 * rows * LANES, transcendentals=0
        ),
    )(view, *done)


def put_gate(out_ref, value, expert, width):
    rows = value.shape[0]
    lane = lax.broadcasted_iota(jnp.int32, (rows, META), 1)
    high = value.astype(BF).astype(F32)
    low = value - high
    pair = jnp.where(lane == expert, high, 0.0)
    pair = jnp.where(lane == expert + EXP_WIN, low, pair)
    out_ref[:, width:] = pair.astype(out_ref.dtype)


def main_kernel(n, owner_ref, *refs):
    pieces, refs = refs[:n], refs[n:]
    low_ref, high_ref, down_ref, tok_ref, grad_ref, pre_ref, hid_ref, prob_ref, own_ref, send_ref = refs
    rows = pieces[0].shape[0]
    width = down_ref.shape[1]
    hid = down_ref.shape[0]
    cut = low_ref.shape[0]
    expert = owner_ref[lax.axis_index("dev")]
    metas = []
    for i in range(0, n, 2):
        pair = [pieces[i][...].astype(F32), pieces[i + 1][...].astype(F32)]
        both = jnp.concatenate(pair, 0)
        here = pl.ds(i * rows, 2 * rows)
        tok_ref[here, :] = both[:, :width].astype(BF)
        grad_ref[here, :] = both[:, width : 2 * width].astype(BF)
        metas.append(both[:, 2 * width :])
    meta = jnp.concatenate(metas, 0)
    lane = lax.broadcasted_iota(jnp.int32, meta.shape, 1)
    routed = jnp.sum(jnp.where(lane == expert, meta, 0.0), 1, keepdims=True)
    prob = jnp.sum(
        jnp.where((lane >= EXP_WIN) & (lane % EXP_WIN == expert), meta, 0.0), 1, keepdims=True
    )
    prob_ref[...] = jnp.broadcast_to(prob, prob_ref.shape)
    projected = jnp.dot(tok_ref[:, :cut], low_ref[...], preferred_element_type=F32)
    projected += jnp.dot(tok_ref[:, cut:], high_ref[...], preferred_element_type=F32)
    gate, up = projected[:, :hid], projected[:, hid:]
    back = lax.dot_general(grad_ref[...], down_ref[...], NT, preferred_element_type=F32)
    logistic = jax.nn.sigmoid(gate)
    activated = gate * logistic
    hidden = (activated * up).astype(BF)
    hid_ref[...] = hidden
    gate_sum = routed * jnp.sum(hidden.astype(F32) * back, 1, keepdims=True)
    hidden_grad = prob * back
    pre_gate = hidden_grad * up * logistic * (1.0 + gate * (1.0 - logistic))
    pre_ref[:, :hid] = pre_gate.astype(BF)
    pre_ref[:, hid:] = (hidden_grad * activated).astype(BF)
    half = n * rows // 2
    put_gate(own_ref, gate_sum[:half], expert, width)
    put_gate(send_ref, gate_sum[half:], expert, width)
    step = cut // 2
    for c in range(0, width, step):
        weights = low_ref if c < cut else high_ref
        start = c if c < cut else c - cut
        part = lax.dot_general(
            pre_ref[...], weights[start : start + step, :], NT, preferred_element_type=F32
        )
        own_ref[:, c : c + step] = part[:half]
        send_ref[:, c : c + step] = part[half:].astype(BF)


def add_kernel(parts, own_ref, *refs):
    got, (keep_ref, *send_refs) = refs[: -parts - 1], refs[-parts:]
    total = own_ref[...]
    for got_ref in got:
        total += got_ref[...].astype(F32)
    rows = keep_ref.shape[0]
    width = total.shape[1] - META
    keep_ref[...] = total[:rows]
    for i, send_ref in enumerate(send_refs, 1):
        here = total[i * rows : (i + 1) * rows]
        send_ref[:, :width] = here[:, :width].astype(BF)
        tail = here[:, width:]
        lane = lax.broadcasted_iota(jnp.int32, tail.shape, 1)
        value = tail + pltpu.roll(tail, META - EXP_WIN, 1)
        high = value.astype(BF).astype(F32)
        low = pltpu.roll(value - high, EXP_WIN, 1)
        pair = jnp.where(lane < EXP_WIN, high, jnp.where(lane < 2 * EXP_WIN, low, 0.0))
        send_ref[:, width:] = pair.astype(BF)


def add_step(own, got, after, parts):
    rows, width = own.shape
    part = rows // parts
    keep, *send = pl.pallas_call(
        functools.partial(add_kernel, parts),
        in_specs=[VMEM] * (1 + len(got)) + [ANY],
        out_specs=[VMEM] * parts,
        out_shape=[jax.ShapeDtypeStruct((part, width), F32)]
        + [jax.ShapeDtypeStruct((part, width), BF)] * (parts - 1),
        compiler_params=params(),
        cost_estimate=pl.CostEstimate(
            flops=rows * width, bytes_accessed=8 * rows * width, transcendentals=0
        ),
    )(own, *got, after)
    return keep, send


def last_kernel(own_ref, got_ref, ids_ref, after_ref, tok_ref, gates_ref):
    total = own_ref[...] + got_ref[...].astype(F32)
    rows = total.shape[0]
    width = total.shape[1] - META
    tok_ref[...] = total[:, :width].astype(BF)
    tail = total[:, width:]
    value = tail + pltpu.roll(tail, META - EXP_WIN, 1)
    lane = lax.broadcasted_iota(jnp.int32, (rows, META), 1)
    diag = lax.broadcasted_iota(jnp.int32, (rows, rows), 0) == lax.broadcasted_iota(
        jnp.int32, (rows, rows), 1
    )
    for k in range(ids_ref.shape[0]):
        ids = jnp.broadcast_to(ids_ref[k : k + 1, :].astype(F32), (rows, rows))
        ids = jnp.sum(jnp.where(diag, ids, 0.0), 1, keepdims=True)
        hit = (lane.astype(F32) == ids) & (lane < EXP_WIN)
        column = jnp.sum(jnp.where(hit, value, 0.0), 1, keepdims=True)
        square = jnp.where(diag, jnp.broadcast_to(column, (rows, rows)), 0.0)
        gates_ref[k : k + 1, :] = jnp.sum(square, 0, keepdims=True)


def win_block(tok_ref, pre_ref, column, out_ref):
    wide = pre_ref.shape[1]
    group = wide // LANES
    per = SIDE // group
    tiles = group // 2
    rows = out_ref.shape[0] // group
    put = shuffle(group, inverse=True)
    block = lax.dot_general(
        tok_ref[:, column : column + rows], pre_ref[...], TN, preferred_element_type=F32
    ).astype(BF)
    for s in range(0, rows // per, 2):
        sides = []
        for half in range(2):
            here = (s + half) * per
            sides.append(
                jnp.concatenate(
                    [
                        block[here : here + per, c * LANES : (c + 1) * LANES]
                        for c in [q % 2 * tiles + q // 2 for q in range(group)]
                    ],
                    0,
                )
            )
        both = jnp.dot(put, jnp.concatenate(sides, 1), preferred_element_type=F32).astype(BF)
        out_ref[s * SIDE : (s + 1) * SIDE, :] = both[:, :LANES]
        out_ref[(s + 1) * SIDE : (s + 2) * SIDE, :] = both[:, LANES:]


def win_kernel(blocks, parity, tok_ref, pre_ref, *refs):
    out_hbm, token_ref, near_ref, sems = refs[-4:]
    size = near_ref.shape[1]
    columns = size * LANES // pre_ref.shape[1]
    token_ref[...] = jnp.zeros_like(token_ref)

    def run(blocks):
        copies = []
        for j, block in enumerate(blocks):
            if j >= 2:
                copies[j - 2].wait()
            win_block(tok_ref, pre_ref, block * columns, near_ref.at[j % 2])
            copies.append(
                pltpu.make_async_copy(
                    near_ref.at[j % 2],
                    out_hbm.at[pl.ds(block * size, size), :],
                    sems.at[j % 2],
                )
            )
            copies[j].start()
        for copy in copies[-2:]:
            copy.wait()

    if parity is None:
        run(blocks)
        return
    odd = lax.axis_index("dev") % 2 == 1
    pl.when(odd)(lambda: run(blocks[1]))
    pl.when(jnp.logical_not(odd))(lambda: run(blocks[0]))


def grad_in(tok, pre, after, blocks, out=None, parity=None, block=512):
    rows, d = tok.shape
    wide = pre.shape[1]
    group = wide // LANES
    count = len(blocks) if parity is None else max(len(b) for b in blocks)
    return pl.pallas_call(
        functools.partial(win_kernel, blocks, parity),
        in_specs=[VMEM, VMEM, ANY] + ([] if out is None else [ANY]),
        out_specs=[ANY, VMEM],
        out_shape=[
            jax.ShapeDtypeStruct((d * group, LANES), BF),
            jax.ShapeDtypeStruct((8, LANES), F32),
        ],
        scratch_shapes=[
            pltpu.VMEM((2, block * group, LANES), BF),
            pltpu.SemaphoreType.DMA((2,)),
        ],
        input_output_aliases={} if out is None else {3: 0},
        compiler_params=params(),
        cost_estimate=pl.CostEstimate(
            flops=2 * rows * count * block * wide,
            bytes_accessed=4 * count * block * wide,
            transcendentals=0,
        ),
    )(tok, pre, after, *([] if out is None else [out]))


def down_kernel(hid_ref, grad_ref, prob_ref, after_ref, out_hbm, token_ref, scaled_ref, near_ref, sems):
    token_ref[...] = jnp.zeros_like(token_ref)
    scaled_ref[...] = (prob_ref[:, :1] * grad_ref[...].astype(F32)).astype(BF)
    count, rows, _ = near_ref.shape
    copies = []
    for j in range(count):
        here = slice(j * rows, (j + 1) * rows)
        near_ref[j] = lax.dot_general(
            hid_ref[:, here], scaled_ref[...], TN, preferred_element_type=F32
        ).astype(BF)
        copies.append(
            pltpu.make_async_copy(
                near_ref.at[j], out_hbm.at[pl.ds(j * rows, rows), :], sems.at[j]
            )
        )
        copies[j].start()
    for copy in copies:
        copy.wait()


def grad_down(hidden, grads, prob, after):
    rows, d = grads.shape
    hid = hidden.shape[1]
    return pl.pallas_call(
        down_kernel,
        in_specs=[VMEM] * 3 + [ANY],
        out_specs=[ANY, VMEM],
        out_shape=[
            jax.ShapeDtypeStruct((hid, d), BF),
            jax.ShapeDtypeStruct((8, LANES), F32),
        ],
        scratch_shapes=[
            pltpu.VMEM((rows, d), BF),
            pltpu.VMEM((hid // LANES, LANES, d), BF),
            pltpu.SemaphoreType.DMA((hid // LANES,)),
        ],
        compiler_params=params(),
        cost_estimate=pl.CostEstimate(
            flops=2 * rows * d * hid, bytes_accessed=4 * d * hid, transcendentals=0
        ),
    )(hidden, grads, prob, after)


def shards(tokens, grad_out, expert_ids, gate_probs, device_expert, w_in, w_down):
    n = lax.axis_size("dev")
    rows, width = tokens.shape
    hid = w_down.shape[0]
    ids_t = expert_ids.T
    probs_t = gate_probs.T
    bits = xor_bits(n)

    own = pl.pallas_call(
        pack_kernel,
        in_specs=[VMEM] * 4,
        out_specs=VMEM,
        out_shape=jax.ShapeDtypeStruct((rows, 2 * width + META), BF),
        compiler_params=params(60),
    )(tokens, grad_out, ids_t, probs_t)

    order = [0]
    for bit in bits:
        order = order + [o ^ bit for o in order]
    view = lane_rows(w_in)
    held = {0: own}
    far, near = n // 2, n // 4
    cross = near + 2

    def piece(o):
        if o not in held:
            bit = near if o == cross else o & -o
            held[o] = xor_swap(piece(o ^ bit), bit)
        return held[o]

    early = split_weights(view, 0, width, 2 * hid, 1)
    held[0], early = lax.optimization_barrier((own, early))
    low = split_weights(view, 0, width, 2 * hid, 0, early)
    high = split_weights(view, 1, width, 2 * hid)
    held[far], low = lax.optimization_barrier((piece(far), low))
    held[far + 2], high = lax.optimization_barrier((piece(far + 2), high))
    weights = [low, high]
    for o in order:
        piece(o)

    total = n * rows
    half = total // 2
    tok, grads, pre, hidden, prob, mine, send = pl.pallas_call(
        functools.partial(main_kernel, n),
        in_specs=[SMEM] + [VMEM] * (n + 3),
        out_specs=[VMEM] * 7,
        out_shape=[
            jax.ShapeDtypeStruct((total, width), BF),
            jax.ShapeDtypeStruct((total, width), BF),
            jax.ShapeDtypeStruct((total, 2 * hid), BF),
            jax.ShapeDtypeStruct((total, hid), BF),
            jax.ShapeDtypeStruct((total, META), F32),
            jax.ShapeDtypeStruct((half, width + META), F32),
            jax.ShapeDtypeStruct((half, width + META), BF),
        ],
        compiler_params=params(),
    )(device_expert, *[held[o] for o in order], *weights, w_down)

    steps = list(range(width // 512))
    got = [xor_swap(send, 1)]
    grad_w_in, after = grad_in(tok, pre, prob, steps[:1])
    mine, (by_near, by_side, by_both) = add_step(mine, got, after, 4)
    got = [xor_swap(by_both, 6), xor_swap(by_side, 2), xor_swap(by_near, 4)]
    grad_w_in, after = grad_in(tok, pre, mine, steps[1:4], grad_w_in)
    grad_w_down, after = grad_down(hidden, grads, prob, after)
    for bit in bits[-4::-1]:
        mine, (send,) = add_step(mine, got, after, 2)
        if bit == 8:
            rest = steps[4:]
            got = [xor_swap(send, bit)]
            grad_w_in, after = grad_in(tok, pre, mine, rest, grad_w_in)
            continue
        got = [xor_swap(send, bit)]
    tiles = hid // LANES
    grad_w_in = grad_w_in.reshape(width, tiles, 2, LANES).transpose(0, 2, 1, 3)
    grad_w_in = grad_w_in.reshape(width, 2, hid)
    grad_tokens, gates_t = pl.pallas_call(
        last_kernel,
        in_specs=[VMEM] * 3 + [ANY],
        out_specs=[VMEM] * 2,
        out_shape=[
            jax.ShapeDtypeStruct((rows, width), BF),
            jax.ShapeDtypeStruct((expert_ids.shape[1], rows), F32),
        ],
        compiler_params=params(),
    )(mine, *got, ids_t, after)
    return grad_tokens, gates_t.T, grad_w_in, grad_w_down


def solution(mesh):
    return jax.shard_map(
        shards,
        mesh=mesh,
        in_specs=(
            P(("parts", "dev"), None),
            P(("parts", "dev"), None),
            P(("parts", "dev"), None),
            P(("parts", "dev"), None),
            P(),
            P(None, None, "dev"),
            P("dev", None),
        ),
        out_specs=(
            P(("parts", "dev"), None),
            P(("parts", "dev"), None),
            P("parts", None, "dev"),
            P(("parts", "dev"), None),
        ),
        check_vma=False,
    )
```

```python
import functools

import jax
import jax.numpy as jnp
from jax import lax
from jax.experimental import pallas as pl
from jax.experimental.pallas import tpu as pltpu
from jax.sharding import PartitionSpec as P

EXP_WIN = 4
META = 128
LANES = 128
SIDE = 256
BF = jnp.bfloat16
F32 = jnp.float32
VMEM = pl.BlockSpec(memory_space=pltpu.VMEM)
ANY = pl.BlockSpec(memory_space=pl.ANY)
SMEM = pl.BlockSpec(memory_space=pltpu.SMEM)
NT = (((1,), (1,)), ((), ()))
TN = (((0,), (0,)), ((), ()))


def params(mib=16):
    return pltpu.CompilerParams(vmem_limit_bytes=mib << 20)


def xor_swap(value, bit):
    n = lax.axis_size("dev")
    other = {2: 4, 4: 2}.get(bit, bit) if n >= 8 else bit
    return lax.ppermute(value, "dev", [(i, i ^ (other if i & 1 else bit)) for i in range(n)])


def xor_bits(n):
    bits = []
    bit = n // 2
    while bit:
        bits.append(bit)
        bit //= 2
    return bits


def pack_kernel(tok_ref, grad_ref, ids_ref, prob_ref, out_ref):
    rows, width = tok_ref.shape
    out_ref[:, :width] = tok_ref[...]
    out_ref[:, width : 2 * width] = grad_ref[...]
    top = ids_ref.shape[0]
    diag = lax.broadcasted_iota(jnp.int32, (rows, rows), 0) == lax.broadcasted_iota(
        jnp.int32, (rows, rows), 1
    )
    lane = lax.broadcasted_iota(jnp.int32, (rows, META), 1)
    expert = lane % EXP_WIN
    flag = jnp.zeros((rows, META), F32)
    prob = jnp.zeros((rows, META), F32)
    for k in range(top):
        ids = jnp.broadcast_to(ids_ref[k : k + 1, :].astype(F32), (rows, rows))
        val = jnp.broadcast_to(prob_ref[k : k + 1, :], (rows, rows))
        ids = jnp.sum(jnp.where(diag, ids, 0.0), 1, keepdims=True)
        val = jnp.sum(jnp.where(diag, val, 0.0), 1, keepdims=True)
        hit = expert.astype(F32) == ids
        flag = jnp.where(hit, 1.0, flag)
        prob = prob + jnp.where(hit, val, 0.0)
    high = prob.astype(BF).astype(F32)
    mid = (prob - high).astype(BF).astype(F32)
    low = prob - high - mid
    part = lane // EXP_WIN
    meta = jnp.where(part == 0, flag, 0.0)
    meta = jnp.where(part == 1, high, meta)
    meta = jnp.where(part == 2, mid, meta)
    meta = jnp.where(part == 3, low, meta)
    out_ref[:, 2 * width :] = meta.astype(BF)


def shuffle(group, inverse=False):
    per = SIDE // group
    row = lax.broadcasted_iota(jnp.int32, (SIDE, SIDE), 0)
    col = lax.broadcasted_iota(jnp.int32, (SIDE, SIDE), 1)
    if inverse:
        row, col = col, row
    return (col == (row % per) * group + row // per).astype(BF)


def split_rows(part, w_hbm, out_ref, w_ref, sems):
    d, wide = out_ref.shape
    group = wide // LANES
    per = SIDE // group
    tiles = group // 2
    take = shuffle(group)
    parts = sems.shape[0]
    size = d * group // parts
    copies = [
        pltpu.make_async_copy(
            w_hbm.at[pl.ds((part * parts + i) * size, size), :],
            w_ref.at[pl.ds(i * size, size), :],
            sems.at[i],
        )
        for i in range(parts)
    ]
    for copy in copies:
        copy.start()
    for s in range(0, d // per, 2):
        if s * SIDE % size == 0:
            copies[s * SIDE // size].wait()
        pair = jnp.concatenate(
            [w_ref[s * SIDE : (s + 1) * SIDE, :], w_ref[(s + 1) * SIDE : (s + 2) * SIDE, :]], 1
        )
        rows = jnp.dot(take, pair, preferred_element_type=F32).astype(BF)
        for q in range(group):
            column = (q % 2 * tiles + q // 2) * LANES
            for half in range(2):
                here = (s + half) * per
                out_ref[here : here + per, column : column + LANES] = rows[
                    q * per : (q + 1) * per, half * LANES : (half + 1) * LANES
                ]


def split_kernel(part, when, w_hbm, *refs):
    done_ref, (out_ref, w_ref, sems) = refs[:-3], refs[-3:]
    if when is None:
        split_rows(part, w_hbm, out_ref, w_ref, sems)
        return
    mine = lax.axis_index("dev") % 2 == when

    @pl.when(mine)
    def _():
        split_rows(part, w_hbm, out_ref, w_ref, sems)

    if done_ref:

        @pl.when(jnp.logical_not(mine))
        def _():
            out_ref[...] = done_ref[0][...]


def lane_rows(w_in):
    d, two, hid = w_in.shape
    tiles = hid // LANES
    return w_in.reshape(d, two, tiles, LANES).transpose(0, 2, 1, 3).reshape(-1, LANES)


def split_weights(view, part, d, wide, when=None, *done):
    rows = view.shape[0] // 2
    return pl.pallas_call(
        functools.partial(split_kernel, part, when),
        in_specs=[ANY] + [VMEM] * len(done),
        out_specs=VMEM,
        out_shape=jax.ShapeDtypeStruct((d // 2, wide), BF),
        scratch_shapes=[pltpu.VMEM((rows, LANES), BF), pltpu.SemaphoreType.DMA((3,))],
        compiler_params=params(50),
        cost_estimate=pl.CostEstimate(
            flops=2 * rows * SIDE * LANES, bytes_accessed=4 * rows * LANES, transcendentals=0
        ),
    )(view, *done)


def put_gate(out_ref, value, expert, width):
    rows = value.shape[0]
    lane = lax.broadcasted_iota(jnp.int32, (rows, META), 1)
    high = value.astype(BF).astype(F32)
    low = value - high
    pair = jnp.where(lane == expert, high, 0.0)
    pair = jnp.where(lane == expert + EXP_WIN, low, pair)
    out_ref[:, width:] = pair.astype(out_ref.dtype)


def main_kernel(n, owner_ref, *refs):
    pieces, refs = refs[:n], refs[n:]
    low_ref, high_ref, down_ref, tok_ref, grad_ref, pre_ref, hid_ref, prob_ref, own_ref, send_ref = refs
    rows = pieces[0].shape[0]
    width = down_ref.shape[1]
    hid = down_ref.shape[0]
    cut = low_ref.shape[0]
    expert = owner_ref[lax.axis_index("dev")]
    metas = []
    for i in range(0, n, 2):
        pair = [pieces[i][...].astype(F32), pieces[i + 1][...].astype(F32)]
        both = jnp.concatenate(pair, 0)
        here = pl.ds(i * rows, 2 * rows)
        tok_ref[here, :] = both[:, :width].astype(BF)
        grad_ref[here, :] = both[:, width : 2 * width].astype(BF)
        metas.append(both[:, 2 * width :])
    meta = jnp.concatenate(metas, 0)
    lane = lax.broadcasted_iota(jnp.int32, meta.shape, 1)
    routed = jnp.sum(jnp.where(lane == expert, meta, 0.0), 1, keepdims=True)
    prob = jnp.sum(
        jnp.where((lane >= EXP_WIN) & (lane % EXP_WIN == expert), meta, 0.0), 1, keepdims=True
    )
    prob_ref[...] = jnp.broadcast_to(prob, prob_ref.shape)
    projected = jnp.dot(tok_ref[:, :cut], low_ref[...], preferred_element_type=F32)
    projected += jnp.dot(tok_ref[:, cut:], high_ref[...], preferred_element_type=F32)
    gate, up = projected[:, :hid], projected[:, hid:]
    back = lax.dot_general(grad_ref[...], down_ref[...], NT, preferred_element_type=F32)
    logistic = jax.nn.sigmoid(gate)
    activated = gate * logistic
    hidden = (activated * up).astype(BF)
    hid_ref[...] = hidden
    gate_sum = routed * jnp.sum(hidden.astype(F32) * back, 1, keepdims=True)
    hidden_grad = prob * back
    pre_gate = hidden_grad * up * logistic * (1.0 + gate * (1.0 - logistic))
    pre_ref[:, :hid] = pre_gate.astype(BF)
    pre_ref[:, hid:] = (hidden_grad * activated).astype(BF)
    half = n * rows // 2
    put_gate(own_ref, gate_sum[:half], expert, width)
    put_gate(send_ref, gate_sum[half:], expert, width)
    step = cut // 2
    for c in range(0, width, step):
        weights = low_ref if c < cut else high_ref
        start = c if c < cut else c - cut
        part = lax.dot_general(
            pre_ref[...], weights[start : start + step, :], NT, preferred_element_type=F32
        )
        own_ref[:, c : c + step] = part[:half]
        send_ref[:, c : c + step] = part[half:].astype(BF)


def add_kernel(parts, own_ref, *refs):
    got, (keep_ref, *send_refs) = refs[: -parts - 1], refs[-parts:]
    total = own_ref[...]
    for got_ref in got:
        total += got_ref[...].astype(F32)
    rows = keep_ref.shape[0]
    width = total.shape[1] - META
    keep_ref[...] = total[:rows]
    for i, send_ref in enumerate(send_refs, 1):
        here = total[i * rows : (i + 1) * rows]
        send_ref[:, :width] = here[:, :width].astype(BF)
        tail = here[:, width:]
        lane = lax.broadcasted_iota(jnp.int32, tail.shape, 1)
        value = tail + pltpu.roll(tail, META - EXP_WIN, 1)
        high = value.astype(BF).astype(F32)
        low = pltpu.roll(value - high, EXP_WIN, 1)
        pair = jnp.where(lane < EXP_WIN, high, jnp.where(lane < 2 * EXP_WIN, low, 0.0))
        send_ref[:, width:] = pair.astype(BF)


def add_step(own, got, after, parts):
    rows, width = own.shape
    part = rows // parts
    keep, *send = pl.pallas_call(
        functools.partial(add_kernel, parts),
        in_specs=[VMEM] * (1 + len(got)) + [ANY],
        out_specs=[VMEM] * parts,
        out_shape=[jax.ShapeDtypeStruct((part, width), F32)]
        + [jax.ShapeDtypeStruct((part, width), BF)] * (parts - 1),
        compiler_params=params(),
        cost_estimate=pl.CostEstimate(
            flops=rows * width, bytes_accessed=8 * rows * width, transcendentals=0
        ),
    )(own, *got, after)
    return keep, send


def last_kernel(own_ref, got_ref, ids_ref, after_ref, tok_ref, gates_ref):
    total = own_ref[...] + got_ref[...].astype(F32)
    rows = total.shape[0]
    width = total.shape[1] - META
    tok_ref[...] = total[:, :width].astype(BF)
    tail = total[:, width:]
    value = tail + pltpu.roll(tail, META - EXP_WIN, 1)
    lane = lax.broadcasted_iota(jnp.int32, (rows, META), 1)
    diag = lax.broadcasted_iota(jnp.int32, (rows, rows), 0) == lax.broadcasted_iota(
        jnp.int32, (rows, rows), 1
    )
    for k in range(ids_ref.shape[0]):
        ids = jnp.broadcast_to(ids_ref[k : k + 1, :].astype(F32), (rows, rows))
        ids = jnp.sum(jnp.where(diag, ids, 0.0), 1, keepdims=True)
        hit = (lane.astype(F32) == ids) & (lane < EXP_WIN)
        column = jnp.sum(jnp.where(hit, value, 0.0), 1, keepdims=True)
        square = jnp.where(diag, jnp.broadcast_to(column, (rows, rows)), 0.0)
        gates_ref[k : k + 1, :] = jnp.sum(square, 0, keepdims=True)


def win_block(tok_ref, pre_ref, column, out_ref):
    wide = pre_ref.shape[1]
    group = wide // LANES
    per = SIDE // group
    tiles = group // 2
    rows = out_ref.shape[0] // group
    put = shuffle(group, inverse=True)
    block = lax.dot_general(
        tok_ref[:, column : column + rows], pre_ref[...], TN, preferred_element_type=F32
    ).astype(BF)
    for s in range(0, rows // per, 2):
        sides = []
        for half in range(2):
            here = (s + half) * per
            sides.append(
                jnp.concatenate(
                    [
                        block[here : here + per, c * LANES : (c + 1) * LANES]
                        for c in [q % 2 * tiles + q // 2 for q in range(group)]
                    ],
                    0,
                )
            )
        both = jnp.dot(put, jnp.concatenate(sides, 1), preferred_element_type=F32).astype(BF)
        out_ref[s * SIDE : (s + 1) * SIDE, :] = both[:, :LANES]
        out_ref[(s + 1) * SIDE : (s + 2) * SIDE, :] = both[:, LANES:]


def win_kernel(blocks, parity, tok_ref, pre_ref, *refs):
    out_hbm, token_ref, near_ref, sems = refs[-4:]
    size = near_ref.shape[1]
    columns = size * LANES // pre_ref.shape[1]
    token_ref[...] = jnp.zeros_like(token_ref)

    def run(blocks):
        copies = []
        for j, block in enumerate(blocks):
            if j >= 2:
                copies[j - 2].wait()
            win_block(tok_ref, pre_ref, block * columns, near_ref.at[j % 2])
            copies.append(
                pltpu.make_async_copy(
                    near_ref.at[j % 2],
                    out_hbm.at[pl.ds(block * size, size), :],
                    sems.at[j % 2],
                )
            )
            copies[j].start()
        for copy in copies[-2:]:
            copy.wait()

    if parity is None:
        run(blocks)
        return
    odd = lax.axis_index("dev") % 2 == 1
    pl.when(odd)(lambda: run(blocks[1]))
    pl.when(jnp.logical_not(odd))(lambda: run(blocks[0]))


def grad_in(tok, pre, after, blocks, out=None, parity=None, block=512):
    rows, d = tok.shape
    wide = pre.shape[1]
    group = wide // LANES
    count = len(blocks) if parity is None else max(len(b) for b in blocks)
    return pl.pallas_call(
        functools.partial(win_kernel, blocks, parity),
        in_specs=[VMEM, VMEM, ANY] + ([] if out is None else [ANY]),
        out_specs=[ANY, VMEM],
        out_shape=[
            jax.ShapeDtypeStruct((d * group, LANES), BF),
            jax.ShapeDtypeStruct((8, LANES), F32),
        ],
        scratch_shapes=[
            pltpu.VMEM((2, block * group, LANES), BF),
            pltpu.SemaphoreType.DMA((2,)),
        ],
        input_output_aliases={} if out is None else {3: 0},
        compiler_params=params(),
        cost_estimate=pl.CostEstimate(
            flops=2 * rows * count * block * wide,
            bytes_accessed=4 * count * block * wide,
            transcendentals=0,
        ),
    )(tok, pre, after, *([] if out is None else [out]))


def down_kernel(hid_ref, grad_ref, prob_ref, after_ref, out_hbm, token_ref, scaled_ref, near_ref, sems):
    token_ref[...] = jnp.zeros_like(token_ref)
    scaled_ref[...] = (prob_ref[:, :1] * grad_ref[...].astype(F32)).astype(BF)
    count, rows, _ = near_ref.shape
    copies = []
    for j in range(count):
        here = slice(j * rows, (j + 1) * rows)
        near_ref[j] = lax.dot_general(
            hid_ref[:, here], scaled_ref[...], TN, preferred_element_type=F32
        ).astype(BF)
        copies.append(
            pltpu.make_async_copy(
                near_ref.at[j], out_hbm.at[pl.ds(j * rows, rows), :], sems.at[j]
            )
        )
        copies[j].start()
    for copy in copies:
        copy.wait()


def grad_down(hidden, grads, prob, after):
    rows, d = grads.shape
    hid = hidden.shape[1]
    return pl.pallas_call(
        down_kernel,
        in_specs=[VMEM] * 3 + [ANY],
        out_specs=[ANY, VMEM],
        out_shape=[
            jax.ShapeDtypeStruct((hid, d), BF),
            jax.ShapeDtypeStruct((8, LANES), F32),
        ],
        scratch_shapes=[
            pltpu.VMEM((rows, d), BF),
            pltpu.VMEM((hid // LANES, LANES, d), BF),
            pltpu.SemaphoreType.DMA((hid // LANES,)),
        ],
        compiler_params=params(),
        cost_estimate=pl.CostEstimate(
            flops=2 * rows * d * hid, bytes_accessed=4 * d * hid, transcendentals=0
        ),
    )(hidden, grads, prob, after)


def shards(tokens, grad_out, expert_ids, gate_probs, device_expert, w_in, w_down):
    n = lax.axis_size("dev")
    rows, width = tokens.shape
    hid = w_down.shape[0]
    ids_t = expert_ids.T
    probs_t = gate_probs.T
    bits = xor_bits(n)

    own = pl.pallas_call(
        pack_kernel,
        in_specs=[VMEM] * 4,
        out_specs=VMEM,
        out_shape=jax.ShapeDtypeStruct((rows, 2 * width + META), BF),
        compiler_params=params(),
    )(tokens, grad_out, ids_t, probs_t)

    order = [0]
    for bit in bits:
        order = order + [o ^ bit for o in order]
    view = lane_rows(w_in)
    held = {0: own}
    far, near = n // 2, n // 4
    cross = near + 2

    def piece(o):
        if o not in held:
            bit = near if o == cross else o & -o
            held[o] = xor_swap(piece(o ^ bit), bit)
        return held[o]

    early = split_weights(view, 0, width, 2 * hid, 0)
    held[0], early = lax.optimization_barrier((own, early))
    low = split_weights(view, 0, width, 2 * hid, 1, early)
    high = split_weights(view, 1, width, 2 * hid)
    held[far], low = lax.optimization_barrier((piece(far), low))
    held[far + 2], high = lax.optimization_barrier((piece(far + 2), high))
    weights = [low, high]
    for o in order:
        piece(o)

    total = n * rows
    half = total // 2
    tok, grads, pre, hidden, prob, mine, send = pl.pallas_call(
        functools.partial(main_kernel, n),
        in_specs=[SMEM] + [VMEM] * (n + 3),
        out_specs=[VMEM] * 7,
        out_shape=[
            jax.ShapeDtypeStruct((total, width), BF),
            jax.ShapeDtypeStruct((total, width), BF),
            jax.ShapeDtypeStruct((total, 2 * hid), BF),
            jax.ShapeDtypeStruct((total, hid), BF),
            jax.ShapeDtypeStruct((total, META), F32),
            jax.ShapeDtypeStruct((half, width + META), F32),
            jax.ShapeDtypeStruct((half, width + META), BF),
        ],
        compiler_params=params(),
    )(device_expert, *[held[o] for o in order], *weights, w_down)

    steps = list(range(width // 512))
    got = [xor_swap(send, 1)]
    grad_w_in, after = grad_in(tok, pre, prob, steps[:1])
    mine, (by_near, by_side, by_both) = add_step(mine, got, after, 4)
    got = [xor_swap(by_both, 6), xor_swap(by_side, 2), xor_swap(by_near, 4)]
    grad_w_in, after = grad_in(tok, pre, mine, steps[1:4], grad_w_in)
    grad_w_down, after = grad_down(hidden, grads, prob, after)
    for bit in bits[-4::-1]:
        mine, (send,) = add_step(mine, got, after, 2)
        if bit == 8:
            rest = steps[4:]
            got = [xor_swap(send, bit)]
            grad_w_in, after = grad_in(tok, pre, mine, rest, grad_w_in)
            continue
        got = [xor_swap(send, bit)]
    tiles = hid // LANES
    grad_w_in = grad_w_in.reshape(width, tiles, 2, LANES).transpose(0, 2, 1, 3)
    grad_w_in = grad_w_in.reshape(width, 2, hid)
    grad_tokens, gates_t = pl.pallas_call(
        last_kernel,
        in_specs=[VMEM] * 3 + [ANY],
        out_specs=[VMEM] * 2,
        out_shape=[
            jax.ShapeDtypeStruct((rows, width), BF),
            jax.ShapeDtypeStruct((expert_ids.shape[1], rows), F32),
        ],
        compiler_params=params(),
    )(mine, *got, ids_t, after)
    return grad_tokens, gates_t.T, grad_w_in, grad_w_down


def solution(mesh):
    return jax.shard_map(
        shards,
        mesh=mesh,
        in_specs=(
            P(("parts", "dev"), None),
            P(("parts", "dev"), None),
            P(("parts", "dev"), None),
            P(("parts", "dev"), None),
            P(),
            P(None, None, "dev"),
            P("dev", None),
        ),
        out_specs=(
            P(("parts", "dev"), None),
            P(("parts", "dev"), None),
            P("parts", None, "dev"),
            P(("parts", "dev"), None),
        ),
        check_vma=False,
    )
```

```python
import functools

import jax
import jax.numpy as jnp
from jax import lax
from jax.experimental import pallas as pl
from jax.experimental.pallas import tpu as pltpu
from jax.sharding import PartitionSpec as P

EXP_WIN = 4
META = 128
LANES = 128
SIDE = 256
BF = jnp.bfloat16
F32 = jnp.float32
VMEM = pl.BlockSpec(memory_space=pltpu.VMEM)
ANY = pl.BlockSpec(memory_space=pl.ANY)
SMEM = pl.BlockSpec(memory_space=pltpu.SMEM)
NT = (((1,), (1,)), ((), ()))
TN = (((0,), (0,)), ((), ()))


def params(mib=20):
    return pltpu.CompilerParams(vmem_limit_bytes=mib << 20)


def xor_swap(value, bit):
    n = lax.axis_size("dev")
    other = {2: 4, 4: 2}.get(bit, bit) if n >= 8 else bit
    return lax.ppermute(value, "dev", [(i, i ^ (other if i & 1 else bit)) for i in range(n)])


def xor_bits(n):
    bits = []
    bit = n // 2
    while bit:
        bits.append(bit)
        bit //= 2
    return bits


def pack_kernel(tok_ref, grad_ref, ids_ref, prob_ref, out_ref):
    rows, width = tok_ref.shape
    out_ref[:, :width] = tok_ref[...]
    out_ref[:, width : 2 * width] = grad_ref[...]
    top = ids_ref.shape[0]
    diag = lax.broadcasted_iota(jnp.int32, (rows, rows), 0) == lax.broadcasted_iota(
        jnp.int32, (rows, rows), 1
    )
    lane = lax.broadcasted_iota(jnp.int32, (rows, META), 1)
    expert = lane % EXP_WIN
    flag = jnp.zeros((rows, META), F32)
    prob = jnp.zeros((rows, META), F32)
    for k in range(top):
        ids = jnp.broadcast_to(ids_ref[k : k + 1, :].astype(F32), (rows, rows))
        val = jnp.broadcast_to(prob_ref[k : k + 1, :], (rows, rows))
        ids = jnp.sum(jnp.where(diag, ids, 0.0), 1, keepdims=True)
        val = jnp.sum(jnp.where(diag, val, 0.0), 1, keepdims=True)
        hit = expert.astype(F32) == ids
        flag = jnp.where(hit, 1.0, flag)
        prob = prob + jnp.where(hit, val, 0.0)
    high = prob.astype(BF).astype(F32)
    mid = (prob - high).astype(BF).astype(F32)
    low = prob - high - mid
    part = lane // EXP_WIN
    meta = jnp.where(part == 0, flag, 0.0)
    meta = jnp.where(part == 1, high, meta)
    meta = jnp.where(part == 2, mid, meta)
    meta = jnp.where(part == 3, low, meta)
    out_ref[:, 2 * width :] = meta.astype(BF)


def shuffle(group, inverse=False):
    per = SIDE // group
    row = lax.broadcasted_iota(jnp.int32, (SIDE, SIDE), 0)
    col = lax.broadcasted_iota(jnp.int32, (SIDE, SIDE), 1)
    if inverse:
        row, col = col, row
    return (col == (row % per) * group + row // per).astype(BF)


def split_rows(part, w_hbm, out_ref, w_ref, sems):
    d, wide = out_ref.shape
    group = wide // LANES
    per = SIDE // group
    tiles = group // 2
    take = shuffle(group)
    parts = sems.shape[0]
    size = d * group // parts
    copies = [
        pltpu.make_async_copy(
            w_hbm.at[pl.ds((part * parts + i) * size, size), :],
            w_ref.at[pl.ds(i * size, size), :],
            sems.at[i],
        )
        for i in range(parts)
    ]
    for copy in copies:
        copy.start()
    for s in range(0, d // per, 2):
        if s * SIDE % size == 0:
            copies[s * SIDE // size].wait()
        pair = jnp.concatenate(
            [w_ref[s * SIDE : (s + 1) * SIDE, :], w_ref[(s + 1) * SIDE : (s + 2) * SIDE, :]], 1
        )
        rows = jnp.dot(take, pair, preferred_element_type=F32).astype(BF)
        for q in range(group):
            column = (q % 2 * tiles + q // 2) * LANES
            for half in range(2):
                here = (s + half) * per
                out_ref[here : here + per, column : column + LANES] = rows[
                    q * per : (q + 1) * per, half * LANES : (half + 1) * LANES
                ]


def split_kernel(part, when, w_hbm, *refs):
    done_ref, (out_ref, w_ref, sems) = refs[:-3], refs[-3:]
    if when is None:
        split_rows(part, w_hbm, out_ref, w_ref, sems)
        return
    me, n = lax.axis_index("dev"), lax.axis_size("dev")
    early = (me % 2 == 0) & (me < 3 * n // 4)
    mine = early if when == 0 else jnp.logical_not(early)

    @pl.when(mine)
    def _():
        split_rows(part, w_hbm, out_ref, w_ref, sems)

    if done_ref:

        @pl.when(jnp.logical_not(mine))
        def _():
            out_ref[...] = done_ref[0][...]


def lane_rows(w_in):
    d, two, hid = w_in.shape
    tiles = hid // LANES
    return w_in.reshape(d, two, tiles, LANES).transpose(0, 2, 1, 3).reshape(-1, LANES)


def split_weights(view, part, d, wide, when=None, *done):
    rows = view.shape[0] // 2
    return pl.pallas_call(
        functools.partial(split_kernel, part, when),
        in_specs=[ANY] + [VMEM] * len(done),
        out_specs=VMEM,
        out_shape=jax.ShapeDtypeStruct((d // 2, wide), BF),
        scratch_shapes=[pltpu.VMEM((rows, LANES), BF), pltpu.SemaphoreType.DMA((3,))],
        compiler_params=params(50),
        cost_estimate=pl.CostEstimate(
            flops=2 * rows * SIDE * LANES, bytes_accessed=4 * rows * LANES, transcendentals=0
        ),
    )(view, *done)


def put_gate(out_ref, value, expert, width):
    rows = value.shape[0]
    lane = lax.broadcasted_iota(jnp.int32, (rows, META), 1)
    high = value.astype(BF).astype(F32)
    low = value - high
    pair = jnp.where(lane == expert, high, 0.0)
    pair = jnp.where(lane == expert + EXP_WIN, low, pair)
    out_ref[:, width:] = pair.astype(out_ref.dtype)


def main_kernel(n, owner_ref, *refs):
    pieces, refs = refs[:n], refs[n:]
    low_ref, high_ref, down_ref, tok_ref, grad_ref, pre_ref, hid_ref, prob_ref, own_ref, send_ref = refs
    rows = pieces[0].shape[0]
    width = down_ref.shape[1]
    hid = down_ref.shape[0]
    cut = low_ref.shape[0]
    expert = owner_ref[lax.axis_index("dev")]
    metas = []
    for i in range(0, n, 2):
        pair = [pieces[i][...].astype(F32), pieces[i + 1][...].astype(F32)]
        both = jnp.concatenate(pair, 0)
        here = pl.ds(i * rows, 2 * rows)
        tok_ref[here, :] = both[:, :width].astype(BF)
        grad_ref[here, :] = both[:, width : 2 * width].astype(BF)
        metas.append(both[:, 2 * width :])
    meta = jnp.concatenate(metas, 0)
    lane = lax.broadcasted_iota(jnp.int32, meta.shape, 1)
    routed = jnp.sum(jnp.where(lane == expert, meta, 0.0), 1, keepdims=True)
    prob = jnp.sum(
        jnp.where((lane >= EXP_WIN) & (lane % EXP_WIN == expert), meta, 0.0), 1, keepdims=True
    )
    prob_ref[...] = jnp.broadcast_to(prob, prob_ref.shape)
    projected = jnp.dot(tok_ref[:, :cut], low_ref[...], preferred_element_type=F32)
    projected += jnp.dot(tok_ref[:, cut:], high_ref[...], preferred_element_type=F32)
    gate, up = projected[:, :hid], projected[:, hid:]
    back = lax.dot_general(grad_ref[...], down_ref[...], NT, preferred_element_type=F32)
    logistic = jax.nn.sigmoid(gate)
    activated = gate * logistic
    hidden = (activated * up).astype(BF)
    hid_ref[...] = hidden
    gate_sum = routed * jnp.sum(hidden.astype(F32) * back, 1, keepdims=True)
    hidden_grad = prob * back
    pre_gate = hidden_grad * up * logistic * (1.0 + gate * (1.0 - logistic))
    pre_ref[:, :hid] = pre_gate.astype(BF)
    pre_ref[:, hid:] = (hidden_grad * activated).astype(BF)
    half = n * rows // 2
    put_gate(own_ref, gate_sum[:half], expert, width)
    put_gate(send_ref, gate_sum[half:], expert, width)
    step = cut // 2
    for c in range(0, width, step):
        weights = low_ref if c < cut else high_ref
        start = c if c < cut else c - cut
        part = lax.dot_general(
            pre_ref[...], weights[start : start + step, :], NT, preferred_element_type=F32
        )
        own_ref[:, c : c + step] = part[:half]
        send_ref[:, c : c + step] = part[half:].astype(BF)


def add_kernel(parts, own_ref, *refs):
    got, (keep_ref, *send_refs) = refs[: -parts - 1], refs[-parts:]
    total = own_ref[...]
    for got_ref in got:
        total += got_ref[...].astype(F32)
    rows = keep_ref.shape[0]
    width = total.shape[1] - META
    keep_ref[...] = total[:rows]
    for i, send_ref in enumerate(send_refs, 1):
        here = total[i * rows : (i + 1) * rows]
        send_ref[:, :width] = here[:, :width].astype(BF)
        tail = here[:, width:]
        lane = lax.broadcasted_iota(jnp.int32, tail.shape, 1)
        value = tail + pltpu.roll(tail, META - EXP_WIN, 1)
        high = value.astype(BF).astype(F32)
        low = pltpu.roll(value - high, EXP_WIN, 1)
        pair = jnp.where(lane < EXP_WIN, high, jnp.where(lane < 2 * EXP_WIN, low, 0.0))
        send_ref[:, width:] = pair.astype(BF)


def add_step(own, got, after, parts):
    rows, width = own.shape
    part = rows // parts
    keep, *send = pl.pallas_call(
        functools.partial(add_kernel, parts),
        in_specs=[VMEM] * (1 + len(got)) + [ANY],
        out_specs=[VMEM] * parts,
        out_shape=[jax.ShapeDtypeStruct((part, width), F32)]
        + [jax.ShapeDtypeStruct((part, width), BF)] * (parts - 1),
        compiler_params=params(),
        cost_estimate=pl.CostEstimate(
            flops=rows * width, bytes_accessed=8 * rows * width, transcendentals=0
        ),
    )(own, *got, after)
    return keep, send


def last_kernel(own_ref, got_ref, ids_ref, after_ref, tok_ref, gates_ref):
    total = own_ref[...] + got_ref[...].astype(F32)
    rows = total.shape[0]
    width = total.shape[1] - META
    tok_ref[...] = total[:, :width].astype(BF)
    tail = total[:, width:]
    value = tail + pltpu.roll(tail, META - EXP_WIN, 1)
    lane = lax.broadcasted_iota(jnp.int32, (rows, META), 1)
    diag = lax.broadcasted_iota(jnp.int32, (rows, rows), 0) == lax.broadcasted_iota(
        jnp.int32, (rows, rows), 1
    )
    for k in range(ids_ref.shape[0]):
        ids = jnp.broadcast_to(ids_ref[k : k + 1, :].astype(F32), (rows, rows))
        ids = jnp.sum(jnp.where(diag, ids, 0.0), 1, keepdims=True)
        hit = (lane.astype(F32) == ids) & (lane < EXP_WIN)
        column = jnp.sum(jnp.where(hit, value, 0.0), 1, keepdims=True)
        square = jnp.where(diag, jnp.broadcast_to(column, (rows, rows)), 0.0)
        gates_ref[k : k + 1, :] = jnp.sum(square, 0, keepdims=True)


def win_block(tok_ref, pre_ref, column, out_ref):
    wide = pre_ref.shape[1]
    group = wide // LANES
    per = SIDE // group
    tiles = group // 2
    rows = out_ref.shape[0] // group
    put = shuffle(group, inverse=True)
    block = lax.dot_general(
        tok_ref[:, column : column + rows], pre_ref[...], TN, preferred_element_type=F32
    ).astype(BF)
    for s in range(0, rows // per, 2):
        sides = []
        for half in range(2):
            here = (s + half) * per
            sides.append(
                jnp.concatenate(
                    [
                        block[here : here + per, c * LANES : (c + 1) * LANES]
                        for c in [q % 2 * tiles + q // 2 for q in range(group)]
                    ],
                    0,
                )
            )
        both = jnp.dot(put, jnp.concatenate(sides, 1), preferred_element_type=F32).astype(BF)
        out_ref[s * SIDE : (s + 1) * SIDE, :] = both[:, :LANES]
        out_ref[(s + 1) * SIDE : (s + 2) * SIDE, :] = both[:, LANES:]


def win_kernel(blocks, parity, tok_ref, pre_ref, *refs):
    out_hbm, token_ref, near_ref, sems = refs[-4:]
    size = near_ref.shape[1]
    columns = size * LANES // pre_ref.shape[1]
    token_ref[...] = jnp.zeros_like(token_ref)

    def run(blocks):
        copies = []
        for j, block in enumerate(blocks):
            if j >= 2:
                copies[j - 2].wait()
            win_block(tok_ref, pre_ref, block * columns, near_ref.at[j % 2])
            copies.append(
                pltpu.make_async_copy(
                    near_ref.at[j % 2],
                    out_hbm.at[pl.ds(block * size, size), :],
                    sems.at[j % 2],
                )
            )
            copies[j].start()
        for copy in copies[-2:]:
            copy.wait()

    if parity is None:
        run(blocks)
        return
    odd = lax.axis_index("dev") % 2 == 1
    pl.when(odd)(lambda: run(blocks[1]))
    pl.when(jnp.logical_not(odd))(lambda: run(blocks[0]))


def grad_in(tok, pre, after, blocks, out=None, parity=None, block=512):
    rows, d = tok.shape
    wide = pre.shape[1]
    group = wide // LANES
    count = len(blocks) if parity is None else max(len(b) for b in blocks)
    return pl.pallas_call(
        functools.partial(win_kernel, blocks, parity),
        in_specs=[VMEM, VMEM, ANY] + ([] if out is None else [ANY]),
        out_specs=[ANY, VMEM],
        out_shape=[
            jax.ShapeDtypeStruct((d * group, LANES), BF),
            jax.ShapeDtypeStruct((8, LANES), F32),
        ],
        scratch_shapes=[
            pltpu.VMEM((2, block * group, LANES), BF),
            pltpu.SemaphoreType.DMA((2,)),
        ],
        input_output_aliases={} if out is None else {3: 0},
        compiler_params=params(),
        cost_estimate=pl.CostEstimate(
            flops=2 * rows * count * block * wide,
            bytes_accessed=4 * count * block * wide,
            transcendentals=0,
        ),
    )(tok, pre, after, *([] if out is None else [out]))


def down_kernel(hid_ref, grad_ref, prob_ref, after_ref, out_hbm, token_ref, scaled_ref, near_ref, sems):
    token_ref[...] = jnp.zeros_like(token_ref)
    scaled_ref[...] = (prob_ref[:, :1] * grad_ref[...].astype(F32)).astype(BF)
    count, rows, _ = near_ref.shape
    copies = []
    for j in range(count):
        here = slice(j * rows, (j + 1) * rows)
        near_ref[j] = lax.dot_general(
            hid_ref[:, here], scaled_ref[...], TN, preferred_element_type=F32
        ).astype(BF)
        copies.append(
            pltpu.make_async_copy(
                near_ref.at[j], out_hbm.at[pl.ds(j * rows, rows), :], sems.at[j]
            )
        )
        copies[j].start()
    for copy in copies:
        copy.wait()


def grad_down(hidden, grads, prob, after):
    rows, d = grads.shape
    hid = hidden.shape[1]
    return pl.pallas_call(
        down_kernel,
        in_specs=[VMEM] * 3 + [ANY],
        out_specs=[ANY, VMEM],
        out_shape=[
            jax.ShapeDtypeStruct((hid, d), BF),
            jax.ShapeDtypeStruct((8, LANES), F32),
        ],
        scratch_shapes=[
            pltpu.VMEM((rows, d), BF),
            pltpu.VMEM((hid // LANES, LANES, d), BF),
            pltpu.SemaphoreType.DMA((hid // LANES,)),
        ],
        compiler_params=params(),
        cost_estimate=pl.CostEstimate(
            flops=2 * rows * d * hid, bytes_accessed=4 * d * hid, transcendentals=0
        ),
    )(hidden, grads, prob, after)


def shards(tokens, grad_out, expert_ids, gate_probs, device_expert, w_in, w_down):
    n = lax.axis_size("dev")
    rows, width = tokens.shape
    hid = w_down.shape[0]
    ids_t = expert_ids.T
    probs_t = gate_probs.T
    bits = xor_bits(n)

    own = pl.pallas_call(
        pack_kernel,
        in_specs=[VMEM] * 4,
        out_specs=VMEM,
        out_shape=jax.ShapeDtypeStruct((rows, 2 * width + META), BF),
        compiler_params=params(),
    )(tokens, grad_out, ids_t, probs_t)

    order = [0]
    for bit in bits:
        order = order + [o ^ bit for o in order]
    view = lane_rows(w_in)
    held = {0: own}
    far, near = n // 2, n // 4
    cross = near + 2

    def piece(o):
        if o not in held:
            bit = near if o == cross else o & -o
            held[o] = xor_swap(piece(o ^ bit), bit)
        return held[o]

    early = split_weights(view, 0, width, 2 * hid, 0)
    held[0], early = lax.optimization_barrier((own, early))
    low = split_weights(view, 0, width, 2 * hid, 1, early)
    high = split_weights(view, 1, width, 2 * hid)
    held[far], low = lax.optimization_barrier((piece(far), low))
    held[far + 2], high = lax.optimization_barrier((piece(far + 2), high))
    weights = [low, high]
    for o in order:
        piece(o)

    total = n * rows
    half = total // 2
    tok, grads, pre, hidden, prob, mine, send = pl.pallas_call(
        functools.partial(main_kernel, n),
        in_specs=[SMEM] + [VMEM] * (n + 3),
        out_specs=[VMEM] * 7,
        out_shape=[
            jax.ShapeDtypeStruct((total, width), BF),
            jax.ShapeDtypeStruct((total, width), BF),
            jax.ShapeDtypeStruct((total, 2 * hid), BF),
            jax.ShapeDtypeStruct((total, hid), BF),
            jax.ShapeDtypeStruct((total, META), F32),
            jax.ShapeDtypeStruct((half, width + META), F32),
            jax.ShapeDtypeStruct((half, width + META), BF),
        ],
        compiler_params=params(),
    )(device_expert, *[held[o] for o in order], *weights, w_down)

    steps = list(range(width // 512))
    got = [xor_swap(send, 1)]
    grad_w_in, after = grad_in(tok, pre, prob, steps[:1])
    mine, (by_near, by_side, by_both) = add_step(mine, got, after, 4)
    got = [xor_swap(by_both, 6), xor_swap(by_side, 2), xor_swap(by_near, 4)]
    grad_w_in, after = grad_in(tok, pre, mine, steps[1:4], grad_w_in)
    grad_w_down, after = grad_down(hidden, grads, prob, after)
    for bit in bits[-4::-1]:
        mine, (send,) = add_step(mine, got, after, 2)
        if bit == 8:
            rest = steps[4:]
            got = [xor_swap(send, bit)]
            grad_w_in, after = grad_in(tok, pre, mine, rest, grad_w_in)
            continue
        got = [xor_swap(send, bit)]
    tiles = hid // LANES
    grad_w_in = grad_w_in.reshape(width, tiles, 2, LANES).transpose(0, 2, 1, 3)
    grad_w_in = grad_w_in.reshape(width, 2, hid)
    grad_tokens, gates_t = pl.pallas_call(
        last_kernel,
        in_specs=[VMEM] * 3 + [ANY],
        out_specs=[VMEM] * 2,
        out_shape=[
            jax.ShapeDtypeStruct((rows, width), BF),
            jax.ShapeDtypeStruct((expert_ids.shape[1], rows), F32),
        ],
        compiler_params=params(),
    )(mine, *got, ids_t, after)
    return grad_tokens, gates_t.T, grad_w_in, grad_w_down


def solution(mesh):
    return jax.shard_map(
        shards,
        mesh=mesh,
        in_specs=(
            P(("parts", "dev"), None),
            P(("parts", "dev"), None),
            P(("parts", "dev"), None),
            P(("parts", "dev"), None),
            P(),
            P(None, None, "dev"),
            P("dev", None),
        ),
        out_specs=(
            P(("parts", "dev"), None),
            P(("parts", "dev"), None),
            P("parts", None, "dev"),
            P(("parts", "dev"), None),
        ),
        check_vma=False,
    )
```
